32 devices in a mesh: grp: 2 (over x), blk: 16 (over z, y, core).
Axes of the slice: x: 2, y: 2, z: 4, core: 2. Of those that a mesh axis runs over, the one named last changes fastest.
Arguments:
- observed: bfloat16 [512, 16384], P(('grp', 'blk')), parts along dimension 0, may hold values from 0.03 to 2.1, as said below
- good_pixel_mask: int32 [512, 16384], P(('grp', 'blk')), parts along dimension 0, may hold values from 0 to 1, as said below
- templates: bfloat16 [512, 65632], P(('grp', 'blk')), parts along dimension 0, may hold values from -6 to 6
- template_kernel_index: int32 [512], P(('grp', 'blk')), parts along dimension 0, may hold values from 0 to 7
- line_spread_table: float32 [8, 97], replicated, may hold values from 0.05 to 1
- exposure_per_row: int32 [512], P('grp'), parts along dimension 0, may hold values from 0 to 255, each once
Outputs:
- ccf: float32 [512, 16384], P('grp', 'blk'), parts along dimension 0
The draws below stay inside these ranges and needn't reach their ends.
There are 2 independent parts, one for each index of `grp`. The reference program is written for one: setup_inputs(seed, part) draws one part's arguments, and reference() takes and returns one part's arrays. A program takes and returns all parts, laid end to end along the dimension named above; an argument that names none is the same for every part. Nothing has to cross between parts.
Inputs may be any that keep to these rules, and one draw needn't show every extreme that they name: observed flux is positive, so masked is above zero exactly on good pixels. `good_pixel_mask`: some pixel columns are bad in every exposure.
All inputs are finite; a program needn't handle non-finite values.
Results may differ from the reference program's by a relative error of at most 0.0015.
Values may be sent and summed in bfloat16 or wider, within the bound.
A program may use at most 128 MiB of HBM per device.

```python
import math
import jax
import jax.numpy as jnp
from jax import lax

PIX = 16384
LAGS = 64
KERNEL_TAPS = 97
KERNEL_COUNT = 8
OBS = 256
NT = 256
HL = 65632


def draw_observed(key, part):
    key_base, key_gain, key_noise = jax.random.split(jax.random.fold_in(key, 11), 3)
    rows = jnp.arange(OBS, dtype=jnp.float32) / OBS
    gain = (0.5 + rows) * jax.random.uniform(key_gain, (OBS,), jnp.float32, 0.8, 1.2)
    base = jnp.exp(jax.random.uniform(key_base, (PIX,), jnp.float32, -2.302585, 0.0))
    noise = jax.random.uniform(key_noise, (OBS, PIX), jnp.float32, -0.15, 0.15)
    flux = base[None, :] * gain[:, None] * (1.0 + noise)
    return flux.astype(jnp.bfloat16)


def draw_good_pixel_mask(key, part):
    key_cols, key_hits = jax.random.split(jax.random.fold_in(key, 23))
    good_cols = jax.random.randint(key_cols, (PIX,), 0, 16) != 0
    good_hits = jax.random.randint(key_hits, (OBS, PIX), 0, 10) != 0
    return (good_cols[None, :] & good_hits).astype(jnp.int32)


def touch_ends(array, stream_key, low, high):
    longest = array.shape.index(max(array.shape))
    spots = []
    for shift in (0, 1):
        where = [jax.random.randint(jax.random.fold_in(stream_key, axis), (), 0, length) for axis, length in enumerate(array.shape)]
        where[longest] = (where[longest] + shift) % array.shape[longest]
        spots.append(tuple(where))
    return array.at[spots[0]].set(low).at[spots[1]].set(high)


def level_of(rng, extent, shards, smallest, high):
    loudness = 1.0
    for position, blocks in shards:
        heights = jax.random.uniform(jax.random.fold_in(jax.random.fold_in(rng, 6), position), (blocks,), jnp.float32, smallest / len(shards), high / len(shards))
        loudness = loudness * jnp.repeat(jnp.exp(heights), extent[position] // blocks).reshape((-1,) + (1,) * (len(extent) - 1 - position))
    return loudness


def normal_values(own_key, extent, deviation, bound, cuts=(), kind=jnp.bfloat16):
    result = jax.random.normal(own_key, extent, jnp.float32) * deviation
    if len(cuts) > 0:
        result = level_of(own_key, extent, cuts, -0.22, 0.18) * result
    return jnp.clip(result, min=-bound, max=bound).astype(kind)


def setup_inputs(seed: int = 0, part: int = 0) -> dict:
    keys = jax.random.split(jax.random.key(seed), 7)
    own_keys = jax.random.split(jax.random.fold_in(keys[6], part), 7)
    observed = draw_observed(jax.random.fold_in(jax.random.fold_in(keys[6], part), 71), part)
    good_pixel_mask = draw_good_pixel_mask(jax.random.fold_in(jax.random.fold_in(keys[6], part), 71), part)
    templates = normal_values(own_keys[2], (NT, HL), 1.0, 6.0, ((0, 16),))
    template_kernel_index = touch_ends(jax.random.randint(own_keys[3], (NT,), 0, KERNEL_COUNT), jax.random.fold_in(own_keys[3], 1), 0, KERNEL_COUNT - 1).astype(jnp.int32)
    line_spread_table = jnp.clip(jnp.exp(jax.random.uniform(keys[4], (KERNEL_COUNT, KERNEL_TAPS), jnp.float32, math.log(0.05), math.log(1.0))), 0.05, 1.0)
    exposure_per_row = jax.random.permutation(own_keys[5], OBS).astype(jnp.int32)
    return {"observed": observed, "good_pixel_mask": good_pixel_mask, "templates": templates, "template_kernel_index": template_kernel_index, "line_spread_table": line_spread_table, "exposure_per_row": exposure_per_row}


def broadened_templates(templates, template_kernel_index, line_spread_table):
    count_t = templates.shape[0]
    kernel_selector = (template_kernel_index[:, None] == jnp.arange(KERNEL_COUNT, dtype=jnp.int32)[None, :]).astype(jnp.float32)
    kernel_weights = jnp.dot(kernel_selector, line_spread_table, precision=lax.Precision.HIGHEST, preferred_element_type=jnp.float32)
    q_count = (KERNEL_TAPS + 3) // 4
    kernel_weights = jnp.pad(kernel_weights, ((0, 0), (0, 4 * q_count - KERNEL_TAPS))).reshape(count_t, q_count, 4)
    phases = templates.reshape(count_t, PIX + 24, 4).transpose(0, 2, 1)
    smoothed_flux = jnp.zeros((count_t, PIX), jnp.float32)
    for q in range(q_count):
        window = phases[:, :, q:q + PIX].astype(jnp.float32)
        smoothed_flux = smoothed_flux + lax.optimization_barrier(jnp.sum(kernel_weights[:, q, :, None] * window, axis=1))
    return smoothed_flux

def reference(observed, good_pixel_mask, templates, template_kernel_index, line_spread_table, exposure_per_row):
    masked = observed * (good_pixel_mask > 0).astype(jnp.bfloat16)
    present = (masked > 0).astype(jnp.float32)
    flux = masked.astype(jnp.float32)
    count = lax.optimization_barrier(jnp.sum(present, axis=0))
    mean = lax.optimization_barrier(jnp.sum(flux, axis=0)) / jnp.maximum(count, 1.0)
    resid = present * (flux - mean[None, :])
    scale = lax.rsqrt(lax.optimization_barrier(jnp.sum(resid * resid, axis=1)) / PIX + 1e-06)
    ready = (resid * scale[:, None]).astype(jnp.bfloat16).astype(jnp.float32)
    smoothed_flux = broadened_templates(templates, template_kernel_index, line_spread_table)
    shaped = (smoothed_flux * lax.rsqrt(lax.optimization_barrier(jnp.sum(smoothed_flux * smoothed_flux, axis=1, keepdims=True)) / PIX + 1e-06)).astype(jnp.bfloat16)
    padded = jnp.pad(shaped, ((0, 0), (LAGS // 2, LAGS // 2)))
    group = math.gcd(NT, 8)
    grouped = padded.reshape(NT // group, group, PIX + LAGS)

    def one_group(panel):
        band = jnp.stack([panel[:, l:l + PIX] for l in range(LAGS)], axis=2).astype(jnp.float32)
        return jnp.einsum('oj,tjl->otl', ready, band)
    cross = lax.map(one_group, grouped)
    cross = cross.transpose(1, 0, 2, 3).reshape(OBS, NT * LAGS) / jnp.float32(math.sqrt(PIX))
    return jnp.zeros_like(cross).at[exposure_per_row].set(cross)
```

```python
import functools
import math

import jax
import jax.numpy as jnp
from jax import lax
from jax.experimental import pallas as pl
from jax.experimental.pallas import tpu as pltpu
from jax.sharding import PartitionSpec as P

PIX = 16384
LAGS = 64
TAPS = 97
KERNELS = 8
Q = 128
R = PIX // Q
BAND = 640
CHUNKS = 8
LEAD = 3
AHEAD = 7
F32 = jnp.float32
BF16 = jnp.bfloat16
MESH = pl.DeviceIdType.MESH
NT_DIMS = (((1,), (1,)), ((), ()))


def template_kernel(index_ref, table_ref, templates_ref, x_ref, bands, chunks, smooth):
    count = templates_ref.shape[0]
    spread_templates(table_ref, templates_ref, bands, chunks)
    smooth_templates(index_ref, bands, chunks, smooth, 0, count, count)
    pack_templates(smooth, x_ref, count)


def spread_templates(table_ref, templates_ref, bands, chunks):
    count = templates_ref.shape[0]
    for k in range(KERNELS):
        row = jnp.concatenate(
            [table_ref[k : k + 1, :], jnp.zeros((1, BAND - TAPS), F32)], axis=1
        )
        row = jnp.broadcast_to(row, (Q, BAND))
        band = pltpu.roll(row, 0, 1, stride=4, stride_axis=0)
        high = band.astype(BF16)
        bands[k, :, :BAND] = high
        bands[k, :, BAND:] = (band - high.astype(F32)).astype(BF16)

    def spread(r, _):
        at = pl.multiple_of(r * (4 * Q), 128)
        piece = templates_ref[:, pl.ds(at, BAND)].astype(F32)
        for i in range(BAND // 128):
            chunks[i, pl.ds(pl.multiple_of(r * count, count), count), :] = piece[
                :, 128 * i : 128 * (i + 1)
            ]
        return 0

    lax.fori_loop(0, R - 1, spread, 0, unroll=8)
    last = (R - 1) * 4 * Q
    left = templates_ref.shape[1] - last
    tail = templates_ref[:, last:].astype(F32)
    tail = jnp.concatenate([tail, jnp.zeros((count, BAND - left), F32)], axis=1)
    for i in range(BAND // 128):
        chunks[i, (R - 1) * count :, :] = tail[:, 128 * i : 128 * (i + 1)]


def smooth_templates(index_ref, bands, chunks, smooth, first, last, count):
    for t in range(first, last):
        rows = [
            chunks[i, pl.ds(t, R, stride=count), :].astype(BF16) for i in range(BAND // 128)
        ]
        rows = jnp.concatenate(rows + rows, axis=1)
        flux = lax.dot_general(
            bands[index_ref[t]], rows, NT_DIMS, preferred_element_type=F32
        )
        total = jnp.sum(flux * flux)
        smooth[pl.ds(t, Q, stride=count), :] = flux * lax.rsqrt(
            jnp.full((1, 1), total) / PIX + 1e-06
        )


def pack_templates(smooth, x_ref, count):
    half = LAGS // 2
    body = smooth[...]
    lane = lax.broadcasted_iota(jnp.int32, (half * count, R), 1)
    x_ref[half * count : (half + Q) * count, :] = body.astype(BF16)
    before = pltpu.roll(body[(Q - half) * count :, :], 1, 1)
    x_ref[: half * count, :] = jnp.where(lane == 0, 0.0, before).astype(BF16)
    after = pltpu.roll(body[: half * count, :], R - 1, 1)
    x_ref[(half + Q) * count :, :] = jnp.where(lane == R - 1, 0.0, after).astype(BF16)


def shape_templates(templates, template_kernel_index, line_spread_table):
    count = templates.shape[0]
    return pl.pallas_call(
        template_kernel,
        out_shape=jax.ShapeDtypeStruct(((Q + LAGS) * count, R), BF16),
        in_specs=[
            pl.BlockSpec(memory_space=pltpu.SMEM),
            pl.BlockSpec(memory_space=pltpu.VMEM),
            pl.BlockSpec(memory_space=pltpu.VMEM),
        ],
        out_specs=pl.BlockSpec(memory_space=pltpu.VMEM),
        scratch_shapes=[
            pltpu.VMEM((KERNELS, Q, 2 * BAND), BF16),
            pltpu.VMEM((BAND // 128, R * count, 128), F32),
            pltpu.VMEM((Q * count, R), F32),
        ],
        compiler_params=pltpu.CompilerParams(vmem_limit_bytes=40 * 2**20),
        cost_estimate=pl.CostEstimate(
            flops=2 * count * Q * R * 2 * BAND, bytes_accessed=6 * 2**20, transcendentals=0
        ),
        name="shape_templates",
    )(template_kernel_index, line_spread_table, templates)


def place_rows(rows_ref, acc, out_ref, count):
    total_rows = rows_ref.shape[1]
    chosen = (
        lax.broadcasted_iota(jnp.int32, (total_rows, total_rows), 0) == rows_ref[...]
    ).astype(BF16)
    both = jnp.concatenate([chosen, chosen], axis=1)
    for t in range(0, count, 2):
        part = jnp.concatenate(
            [
                jnp.concatenate(
                    [
                        acc[h, pl.ds(t + i, LAGS, stride=count), :]
                        for h in range(total_rows // 128)
                    ],
                    axis=1,
                )
                for i in range(2)
            ],
            axis=0,
        ) * F32(1.0 / math.sqrt(PIX))
        high = part.astype(BF16)
        low = (part - high.astype(F32)).astype(BF16)
        out_ref[:, t * LAGS : (t + 2) * LAGS] = lax.dot_general(
            both,
            jnp.concatenate([high, low], axis=1),
            NT_DIMS,
            preferred_element_type=F32,
        )


def correlate_kernel(step_q, rows_ref, x_ref, g_ref, out_ref, acc):
    step = pl.program_id(0)
    total_rows = rows_ref.shape[1]
    count = x_ref.shape[0] // (Q + LAGS)
    tile = 256

    @pl.when(step == 0)
    def _():
        acc[...] = jnp.zeros_like(acc)

    right = jnp.concatenate([g_ref[i] for i in range(step_q)], axis=1)
    for m in range(LAGS * count // tile):
        left = jnp.concatenate(
            [
                x_ref[pl.ds(pl.multiple_of((step * step_q + i) * count + m * tile, 16), tile), :]
                for i in range(step_q)
            ],
            axis=1,
        )
        part = lax.dot_general(left, right, NT_DIMS, preferred_element_type=F32)
        for h in range(total_rows // 128):
            acc[h, m * tile : (m + 1) * tile, :] += part[:, 128 * h : 128 * (h + 1)]

    @pl.when(step == pl.num_programs(0) - 1)
    def _():
        place_rows(rows_ref, acc, out_ref, count)


def correlate(x, gathered, exposure_per_row):
    total_rows = gathered.shape[1]
    count = x.shape[0] // (Q + LAGS)
    step_q = 8
    return pl.pallas_call(
        functools.partial(correlate_kernel, step_q),
        grid=(Q // step_q,),
        out_shape=jax.ShapeDtypeStruct((total_rows, count * LAGS), F32),
        in_specs=[
            pl.BlockSpec((1, total_rows), lambda s: (0, 0)),
            pl.BlockSpec(x.shape, lambda s: (0, 0)),
            pl.BlockSpec((step_q, total_rows, R), lambda s: (s, 0, 0)),
        ],
        out_specs=pl.BlockSpec((total_rows, count * LAGS), lambda s: (0, 0)),
        scratch_shapes=[pltpu.VMEM((total_rows // 128, LAGS * count, 128), F32)],
        compiler_params=pltpu.CompilerParams(vmem_limit_bytes=40 * 2**20),
        name="correlate",
    )(exposure_per_row.reshape(1, total_rows), x, gathered)


def column_sums(mine, psum):
    kind = lax.broadcasted_iota(jnp.int32, (16, 256), 0)
    lane = lax.broadcasted_iota(jnp.int32, (16, 256), 1)
    pick = (lane // 16 == kind).astype(BF16)
    for j in range(Q // 16):
        part = mine[16 * j : 16 * (j + 1)].reshape(256, R)
        good = (part.astype(F32) > 0).astype(BF16)
        for i, what in enumerate((part, good)):
            psum[j // 4, i, 16 * (j % 4) : 16 * (j % 4 + 1), :] = lax.dot_general(
                pick, what, (((1,), (0,)), ((), ())), preferred_element_type=F32
            )


def row_scales(mine, means):
    zero = jnp.zeros((16, R), F32)

    def add(j, total):
        for i in range(16):
            flux = mine[16 * j + i].astype(F32)
            resid = jnp.where(flux > 0, flux - means[j, i : i + 1, :], 0.0)
            total = total + resid * resid
        return total

    total = lax.fori_loop(0, Q // 16, add, zero)
    return lax.rsqrt(jnp.sum(total, axis=1, keepdims=True) / PIX + 1e-06)


def diagonal():
    row = lax.broadcasted_iota(jnp.int32, (16, R), 0)
    lane = lax.broadcasted_iota(jnp.int32, (16, R), 1)
    return row == lane


def store_body(smooth, x, count):
    x[0, LAGS // 2 : LAGS // 2 + Q] = smooth[...].reshape(Q, count, R).astype(BF16)


def store_margins(x, tt):
    half = LAGS // 2
    count = x.shape[2]
    lane = lax.broadcasted_iota(jnp.int32, (half * count, R), 1)

    def rolled(first, shift, edge):
        part = x[tt, first : first + half].reshape(half * count, R).astype(F32)
        part = jnp.where(lane == edge, 0.0, pltpu.roll(part, shift, 1))
        return part.astype(BF16).reshape(half, count, R)

    x[tt, :half] = rolled(Q, 1, 0)
    x[tt, half + Q :] = rolled(half, R - 1, R - 1)


def cross_kernel(
    mine,
    index_ref,
    table_ref,
    templates_ref,
    out_ref,
    raw,
    ready,
    x,
    partner,
    psum,
    tsum,
    csum,
    rsum,
    means,
    row_scale,
    scale,
    bands,
    chunks,
    smooth,
    raw_send,
    raw_recv,
    x_sem,
    r_send,
    r_recv,
    t_sem,
    s_send,
    s_recv,
    m_send,
    m_recv,
    v_send,
    v_recv,
):
    me = lax.axis_index("blk")
    z, y, c = me // 4, (me // 2) % 2, me % 2
    planes = 4
    count = templates_ref.shape[0]
    span = Q // CHUNKS

    def blk(zz, yy, cc):
        return (zz * 2 + yy) * 2 + cc

    up, down = blk(z + 1, y, c), blk(z - 1, y, c)
    beside, twin = blk(z, 1 - y, c), blk(z, y, 1 - c)
    middle = (z == 1) | (z == 2)
    has_up, has_down = z < planes - 1, z > 0

    def remote(src, dst, send, recv, to):
        return pltpu.make_async_remote_copy(
            src_ref=src,
            dst_ref=dst,
            send_sem=send,
            recv_sem=recv,
            device_id={"blk": to},
            device_id_type=MESH,
        )

    barrier = pltpu.get_barrier_semaphore()

    def greet(o, _):
        pl.semaphore_signal(
            barrier, inc=1, device_id={"blk": lax.rem(me + o, 16)}, device_id_type=MESH
        )
        return 0

    lax.fori_loop(1, 16, greet, 0)
    raw[z, c] = mine[...]
    pl.semaphore_wait(barrier, 15)

    def raw_copy(zs, k, kind, to):
        part = raw.at[zs, c, pl.ds(k * span, span)]
        return remote(
            part, part, raw_send.at[kind, zs, k], raw_recv.at[zs * 2 + c, k], to
        )

    def from_twin(zs, k):
        part = raw.at[zs, 1 - c, pl.ds(k * span, span)]
        remote(
            part, part, raw_send.at[2, zs, k], raw_recv.at[zs * 2 + 1 - c, k], twin
        ).wait_recv()

    def on_sides(h, act):
        for sign in (1, -1):
            zs = z + sign * h
            pl.when((zs >= 0) & (zs < planes))(functools.partial(act, zs, sign))

    def send(s):
        h, k = s // CHUNKS, s % CHUNKS
        if h == 0:
            pl.when(has_up)(lambda: raw_copy(z, k, 0, up).start())
            pl.when(has_down)(lambda: raw_copy(z, k, 1, down).start())
            raw_copy(z, k, 2, twin).start()
        elif h < planes - 1:

            def onward(zs, sign):
                if sign > 0:
                    pl.when(has_down)(lambda: raw_copy(zs, k, 1, down).start())
                else:
                    pl.when(has_up)(lambda: raw_copy(zs, k, 0, up).start())

            on_sides(h, onward)

    def arrive(s):
        h, k = s // CHUNKS + 1, s % CHUNKS

        def land(zs, sign):
            raw_copy(zs, k, 2, twin).wait_recv()
            raw_copy(zs, k, 2, twin).start()

        on_sides(h, land)

    def step(s):
        arrive(s)
        send(s + LEAD)

    for s in range(LEAD):
        send(s)

    column_sums(mine, psum)
    to_twin = remote(psum.at[1 - c], tsum, t_sem.at[0], t_sem.at[1], twin)
    to_twin.start()
    spread_templates(table_ref, templates_ref, bands, chunks)

    def owner(w):
        return blk(1 + w // 2, w % 2, c)

    def sum_copy(w):
        return remote(
            csum.at[w], rsum.at[z * 2 + y], s_send.at[w], s_recv.at[z * 2 + y], owner(w)
        )

    def sum_from(i):
        return remote(csum.at[0], rsum.at[i], s_send.at[0], s_recv.at[i], twin)

    def mean_copy(w, o):
        part = means.at[4 * c + w]
        chip = lax.rem(z * 2 + y + o, 8)
        return remote(
            part, part, m_send.at[o], m_recv.at[w], blk(chip // 2, chip % 2, c)
        )

    mine_w = (z - 1) * 2 + y

    def sums_to_owners():
        to_twin.wait_recv()
        for w in range(4):
            rows = slice(16 * w, 16 * (w + 1))
            csum[w] = psum[c, :, rows, :] + tsum[:, rows, :]
            away = jnp.logical_not(middle & (mine_w == w))
            pl.when(away)(lambda: sum_copy(w).start())

            @pl.when(jnp.logical_not(away))
            def _():
                rsum[z * 2 + y] = csum[w]

    def means_from_owner():
        @pl.when(middle)
        def _():
            for i in range(8):
                pl.when(z * 2 + y != i)(lambda: sum_from(i).wait_recv())
            total = rsum[0]
            for i in range(1, 8):
                total = total + rsum[i]
            means[4 * c + mine_w] = total[0] / jnp.maximum(total[1], 1.0)
            for o in range(1, 8):
                mean_copy(mine_w, o).start()

    half_means = remote(
        means.at[pl.ds(4 * c, 4)],
        means.at[pl.ds(4 * c, 4)],
        t_sem.at[2],
        t_sem.at[3],
        twin,
    )

    def means_to_twin():
        for w in range(4):
            away = jnp.logical_not(middle & (mine_w == w))
            pl.when(away)(lambda: mean_copy(w, 1).wait_recv())
        half_means.start()

    def scale_copy(o):
        at = lax.rem(z * 2 + c + o, 8)
        return remote(
            row_scale.at[z * 2 + c],
            row_scale.at[z * 2 + c],
            v_send.at[o],
            v_recv.at[z * 2 + c],
            blk(at // 2, y, at % 2),
        )

    def scales_out():
        half_means.wait_recv()
        own = row_scales(mine, means)
        row_scale[z * 2 + c] = jnp.sum(
            jnp.where(diagonal(), own, 0.0), axis=0, keepdims=True
        )
        for o in range(1, 8):
            scale_copy(o).start()

    def scales_in():
        for i in range(8):
            part = row_scale.at[i]
            pl.when(z * 2 + c != i)(
                lambda: remote(part, part, v_send.at[0], v_recv.at[i], twin).wait_recv()
            )
            column = jnp.sum(
                jnp.where(diagonal(), row_scale[i], 0.0), axis=1, keepdims=True
            )
            scale[i] = jnp.broadcast_to(column, (16, R))

    x_copy = remote(
        x.at[0, pl.ds(LAGS // 2, Q)],
        x.at[1, pl.ds(LAGS // 2, Q)],
        x_sem.at[0],
        x_sem.at[1],
        beside,
    )

    after = {2: sums_to_owners, 8: means_from_owner, 12: means_to_twin}
    for t in range(0, count, 2):
        smooth_templates(index_ref, bands, chunks, smooth, t, t + 2, count)
        step(t // 2)
        after.get(t + 2, lambda: None)()
    store_body(smooth, x, count)
    x_copy.start()
    scales_out()
    for zs in range(planes):
        ready[zs, :AHEAD] = jnp.zeros((AHEAD, 32, R), BF16)
        ready[zs, AHEAD + Q :] = jnp.zeros((ready.shape[1] - AHEAD - Q, 32, R), BF16)
    store_margins(x, 0)
    step(8)

    def normalise(zs, first, last):
        for cc in range(2):
            factor = scale[zs * 2 + cc]

            def tile(j, _):
                for i in range(16):
                    flux = raw[zs, cc, 16 * j + i].astype(F32)
                    resid = jnp.where(flux > 0, flux - means[j, i : i + 1, :], 0.0)
                    ready[zs, AHEAD + 16 * j + i, 16 * cc : 16 * (cc + 1), :] = (
                        resid * factor
                    ).astype(BF16)
                return 0

            lax.fori_loop(first, last, tile, 0)

    def product(zs, quarter):
        first = 32 * quarter
        width = 32 if quarter < 3 else 40
        right = jnp.concatenate(
            [ready[zs, first + i : first + i + 8].reshape(256, R) for i in range(width)],
            axis=1,
        )
        left = jnp.concatenate(
            [
                jnp.concatenate(
                    [x[tt, first + i + 8 * a] for tt in range(2) for a in range(8)], axis=0
                )
                for i in range(width)
            ],
            axis=1,
        )
        part = lax.dot_general(left, right, NT_DIMS, preferred_element_type=F32)
        if quarter == 0:
            out_ref[zs * 2 + y] = part[:128]
            partner[zs] = part[128:]
        else:
            out_ref[zs * 2 + y] += part[:128]
            partner[zs] += part[128:]

    def result_copy(zs):
        return remote(
            partner.at[zs], out_ref.at[zs * 2 + y], r_send.at[zs], r_recv.at[zs], beside
        )

    def slot(i):
        if isinstance(i, int) and i == 3:
            return jnp.where(z < 2, 3, 0)
        near = jnp.where(z < 2, z + 1, z - 1)
        far = jnp.where(z == 0, 2, jnp.where(z == 1, 0, jnp.where(z == 2, 3, 1)))
        return jnp.where(i == 0, z, jnp.where(i == 1, near, far))

    def all_from_twin(zs):
        for k in range(CHUNKS):
            from_twin(zs, k)

    def whole(i, _):
        zs = slot(i)
        for quarter in range(4):
            product(zs, quarter)
        result_copy(zs).start()
        return 0

    def prepare(i):
        all_from_twin(slot(i))
        normalise(slot(i), 0, Q // 16)

    step(9)
    step(10)
    scales_in()
    prepare(0)
    step(11)
    prepare(1)
    for s in range(12, 16):
        step(s)
    x_copy.wait_recv()
    store_margins(x, 1)
    lax.fori_loop(0, 2, whole, 0)
    prepare(2)
    lax.fori_loop(2, 3, whole, 0)
    last = slot(3)
    for quarter in range(4):
        for s in range(16 + 2 * quarter, 18 + 2 * quarter):
            step(s)
        for k in range(2 * quarter, 2 * quarter + 2):
            from_twin(last, k)
        normalise(last, 2 * quarter, 2 * quarter + 2)
        product(last, quarter)
    result_copy(last).start()

    x_copy.wait_send()
    to_twin.wait_send()
    half_means.wait_send()
    for w in range(4):
        away = jnp.logical_not(middle & (mine_w == w))
        pl.when(away)(lambda: sum_copy(w).wait_send())

    @pl.when(middle)
    def _():
        for o in range(1, 8):
            mean_copy(mine_w, o).wait_send()

    for o in range(1, 8):
        scale_copy(o).wait_send()

    def sent(k, _):
        for zs in range(planes):
            raw_copy(zs, k, 2, twin).wait_send()
            pl.when(has_up & (zs <= z))(lambda: raw_copy(zs, k, 0, up).wait_send())
            pl.when(has_down & (zs >= z))(lambda: raw_copy(zs, k, 1, down).wait_send())
        return 0

    lax.fori_loop(0, CHUNKS, sent, 0)
    for zs in range(planes):
        result_copy(zs).wait_send()
    for zs in range(planes):
        result_copy(zs).wait_recv()


def cross(masked, templates, template_kernel_index, line_spread_table):
    count = templates.shape[0]
    rows = masked.shape[1]
    vmem = pl.BlockSpec(memory_space=pltpu.VMEM)
    dma = pltpu.SemaphoreType.DMA
    return pl.pallas_call(
        cross_kernel,
        out_shape=jax.ShapeDtypeStruct((8, 8 * count, 256), F32),
        in_specs=[vmem, pl.BlockSpec(memory_space=pltpu.SMEM), vmem, vmem],
        out_specs=vmem,
        scratch_shapes=[
            pltpu.VMEM((4, 2, Q, rows, R), BF16),
            pltpu.VMEM((4, Q + 16, 2 * rows, R), BF16),
            pltpu.VMEM((2, Q + LAGS, count, R), BF16),
            pltpu.VMEM((4, 8 * count, 256), F32),
            pltpu.VMEM((2, 2, Q // 2, R), F32),
            pltpu.VMEM((2, Q // 2, R), F32),
            pltpu.VMEM((4, 2, 16, R), F32),
            pltpu.VMEM((8, 2, 16, R), F32),
            pltpu.VMEM((8, 16, R), F32),
            pltpu.VMEM((8, 1, R), F32),
            pltpu.VMEM((8, 16, R), F32),
            pltpu.VMEM((KERNELS, Q, 2 * BAND), BF16),
            pltpu.VMEM((BAND // 128, R * count, 128), F32),
            pltpu.VMEM((Q * count, R), F32),
            dma((3, 4, CHUNKS)),
            dma((8, CHUNKS)),
            dma((2,)),
            dma((4,)),
            dma((4,)),
            dma((4,)),
            dma((4,)),
            dma((8,)),
            dma((8,)),
            dma((4,)),
            dma((8,)),
            dma((8,)),
        ],
        compiler_params=pltpu.CompilerParams(
            collective_id=0, has_side_effects=True, vmem_limit_bytes=48 * 2**20
        ),
        name="cross",
    )(masked, template_kernel_index, line_spread_table, templates)


def place_kernel(rows_ref, part_ref, out_ref, split):
    count = part_ref.shape[1] // 8
    lane = lax.broadcasted_iota(jnp.int32, (8 * count, 128), 1) // 32
    for h in range(2):
        for b in range(8):
            at = 7 - b
            piece = None
            for i in range(4):
                one = part_ref[4 * h + i, :, 128 * (at // 4) : 128 * (at // 4 + 1)]
                shift = 32 * (i - at % 4) % 128
                one = pltpu.roll(one, shift, 1) if shift else one
                piece = one if piece is None else jnp.where(lane == i, one, piece)
            for a in range(8):
                split[h, (8 * a + b) * count : (8 * a + b + 1) * count, :] = piece[
                    a * count : (a + 1) * count
                ]
    place_rows(rows_ref, split, out_ref, count)


def place(parts, exposure_per_row):
    total_rows = 32 * parts.shape[0]
    across = parts.shape[1] * 8
    return pl.pallas_call(
        place_kernel,
        out_shape=jax.ShapeDtypeStruct((total_rows, across), F32),
        in_specs=[pl.BlockSpec(memory_space=pltpu.VMEM)] * 2,
        out_specs=pl.BlockSpec(memory_space=pltpu.VMEM),
        scratch_shapes=[pltpu.VMEM((total_rows // 128, across, 128), F32)],
        compiler_params=pltpu.CompilerParams(vmem_limit_bytes=16 * 2**20),
        name="place",
    )(exposure_per_row.reshape(1, total_rows), parts)


def shards(
    devices,
    observed,
    good_pixel_mask,
    templates,
    template_kernel_index,
    line_spread_table,
    exposure_per_row,
):
    rows = observed.shape[0]
    flux = jnp.where(good_pixel_mask > 0, observed, 0)
    if devices == 16 and rows == 16 and templates.shape[0] == 16:
        masked = flux.reshape(rows, R, Q).transpose(2, 0, 1)
        parts = cross(masked, templates, template_kernel_index, line_spread_table)
        return place(parts, exposure_per_row)
    flux = flux.astype(F32)
    present = (flux > 0).astype(F32)
    sums, counts = jnp.sum(flux, axis=0), jnp.sum(present, axis=0)
    x = shape_templates(templates, template_kernel_index, line_spread_table)
    sums = lax.psum(jnp.stack([sums, counts]), "blk")
    mean = sums[0] / jnp.maximum(sums[1], 1.0)
    resid = present * (flux - mean[None, :])
    scale = lax.rsqrt(jnp.sum(resid * resid, axis=1) / PIX + 1e-06)
    ready = (resid * scale[:, None]).astype(BF16)
    ready = ready.reshape(rows, R, Q).transpose(2, 0, 1)
    gathered = lax.all_gather(ready, "blk", axis=1, tiled=True)
    return correlate(x, gathered, exposure_per_row)


def solution(mesh):
    in_specs = (
        P(("grp", "blk"), None),
        P(("grp", "blk"), None),
        P(("grp", "blk"), None),
        P(("grp", "blk")),
        P(),
        P("grp"),
    )
    out_specs = P("grp", "blk")
    return jax.shard_map(
        functools.partial(shards, mesh.shape["blk"]),
        mesh=mesh,
        in_specs=in_specs,
        out_specs=out_specs,
        check_vma=False,
    )
```

```python
import functools
import math

import jax
import jax.numpy as jnp
from jax import lax
from jax.experimental import pallas as pl
from jax.experimental.pallas import tpu as pltpu
from jax.sharding import PartitionSpec as P

PIX = 16384
LAGS = 64
TAPS = 97
KERNELS = 8
Q = 128
R = PIX // Q
BAND = 640
CHUNKS = 8
LEAD = 3
AHEAD = 7
F32 = jnp.float32
BF16 = jnp.bfloat16
MESH = pl.DeviceIdType.MESH
NT_DIMS = (((1,), (1,)), ((), ()))


def template_kernel(index_ref, table_ref, templates_ref, x_ref, bands, chunks, smooth):
    count = templates_ref.shape[0]
    spread_templates(table_ref, templates_ref, bands, chunks)
    smooth_templates(index_ref, bands, chunks, smooth, 0, count, count)
    pack_templates(smooth, x_ref, count)


def spread_templates(table_ref, templates_ref, bands, chunks):
    count = templates_ref.shape[0]
    for k in range(KERNELS):
        row = jnp.concatenate(
            [table_ref[k : k + 1, :], jnp.zeros((1, BAND - TAPS), F32)], axis=1
        )
        row = jnp.broadcast_to(row, (Q, BAND))
        band = pltpu.roll(row, 0, 1, stride=4, stride_axis=0)
        high = band.astype(BF16)
        bands[k, :, :BAND] = high
        bands[k, :, BAND:] = (band - high.astype(F32)).astype(BF16)

    def spread(r, _):
        at = pl.multiple_of(r * (4 * Q), 128)
        piece = templates_ref[:, pl.ds(at, BAND)].astype(F32)
        for i in range(BAND // 128):
            chunks[i, pl.ds(pl.multiple_of(r * count, count), count), :] = piece[
                :, 128 * i : 128 * (i + 1)
            ]
        return 0

    lax.fori_loop(0, R - 1, spread, 0, unroll=8)
    last = (R - 1) * 4 * Q
    left = templates_ref.shape[1] - last
    tail = templates_ref[:, last:].astype(F32)
    tail = jnp.concatenate([tail, jnp.zeros((count, BAND - left), F32)], axis=1)
    for i in range(BAND // 128):
        chunks[i, (R - 1) * count :, :] = tail[:, 128 * i : 128 * (i + 1)]


def smooth_templates(index_ref, bands, chunks, smooth, first, last, count):
    for t in range(first, last):
        rows = [
            chunks[i, pl.ds(t, R, stride=count), :].astype(BF16) for i in range(BAND // 128)
        ]
        rows = jnp.concatenate(rows + rows, axis=1)
        flux = lax.dot_general(
            bands[index_ref[t]], rows, NT_DIMS, preferred_element_type=F32
        )
        total = jnp.sum(flux * flux)
        smooth[pl.ds(t, Q, stride=count), :] = flux * lax.rsqrt(
            jnp.full((1, 1), total) / PIX + 1e-06
        )


def pack_templates(smooth, x_ref, count):
    half = LAGS // 2
    body = smooth[...]
    lane = lax.broadcasted_iota(jnp.int32, (half * count, R), 1)
    x_ref[half * count : (half + Q) * count, :] = body.astype(BF16)
    before = pltpu.roll(body[(Q - half) * count :, :], 1, 1)
    x_ref[: half * count, :] = jnp.where(lane == 0, 0.0, before).astype(BF16)
    after = pltpu.roll(body[: half * count, :], R - 1, 1)
    x_ref[(half + Q) * count :, :] = jnp.where(lane == R - 1, 0.0, after).astype(BF16)


def shape_templates(templates, template_kernel_index, line_spread_table):
    count = templates.shape[0]
    return pl.pallas_call(
        template_kernel,
        out_shape=jax.ShapeDtypeStruct(((Q + LAGS) * count, R), BF16),
        in_specs=[
            pl.BlockSpec(memory_space=pltpu.SMEM),
            pl.BlockSpec(memory_space=pltpu.VMEM),
            pl.BlockSpec(memory_space=pltpu.VMEM),
        ],
        out_specs=pl.BlockSpec(memory_space=pltpu.VMEM),
        scratch_shapes=[
            pltpu.VMEM((KERNELS, Q, 2 * BAND), BF16),
            pltpu.VMEM((BAND // 128, R * count, 128), F32),
            pltpu.VMEM((Q * count, R), F32),
        ],
        compiler_params=pltpu.CompilerParams(vmem_limit_bytes=40 * 2**20),
        cost_estimate=pl.CostEstimate(
            flops=2 * count * Q * R * 2 * BAND, bytes_accessed=6 * 2**20, transcendentals=0
        ),
        name="shape_templates",
    )(template_kernel_index, line_spread_table, templates)


def place_rows(rows_ref, acc, out_ref, count):
    total_rows = rows_ref.shape[1]
    chosen = (
        lax.broadcasted_iota(jnp.int32, (total_rows, total_rows), 0) == rows_ref[...]
    ).astype(BF16)
    both = jnp.concatenate([chosen, chosen], axis=1)
    for t in range(0, count, 2):
        part = jnp.concatenate(
            [
                jnp.concatenate(
                    [
                        acc[h, pl.ds(t + i, LAGS, stride=count), :]
                        for h in range(total_rows // 128)
                    ],
                    axis=1,
                )
                for i in range(2)
            ],
            axis=0,
        ) * F32(1.0 / math.sqrt(PIX))
        high = part.astype(BF16)
        low = (part - high.astype(F32)).astype(BF16)
        out_ref[:, t * LAGS : (t + 2) * LAGS] = lax.dot_general(
            both,
            jnp.concatenate([high, low], axis=1),
            NT_DIMS,
            preferred_element_type=F32,
        )


def correlate_kernel(step_q, rows_ref, x_ref, g_ref, out_ref, acc):
    step = pl.program_id(0)
    total_rows = rows_ref.shape[1]
    count = x_ref.shape[0] // (Q + LAGS)
    tile = 256

    @pl.when(step == 0)
    def _():
        acc[...] = jnp.zeros_like(acc)

    right = jnp.concatenate([g_ref[i] for i in range(step_q)], axis=1)
    for m in range(LAGS * count // tile):
        left = jnp.concatenate(
            [
                x_ref[pl.ds(pl.multiple_of((step * step_q + i) * count + m * tile, 16), tile), :]
                for i in range(step_q)
            ],
            axis=1,
        )
        part = lax.dot_general(left, right, NT_DIMS, preferred_element_type=F32)
        for h in range(total_rows // 128):
            acc[h, m * tile : (m + 1) * tile, :] += part[:, 128 * h : 128 * (h + 1)]

    @pl.when(step == pl.num_programs(0) - 1)
    def _():
        place_rows(rows_ref, acc, out_ref, count)


def correlate(x, gathered, exposure_per_row):
    total_rows = gathered.shape[1]
    count = x.shape[0] // (Q + LAGS)
    step_q = 8
    return pl.pallas_call(
        functools.partial(correlate_kernel, step_q),
        grid=(Q // step_q,),
        out_shape=jax.ShapeDtypeStruct((total_rows, count * LAGS), F32),
        in_specs=[
            pl.BlockSpec((1, total_rows), lambda s: (0, 0)),
            pl.BlockSpec(x.shape, lambda s: (0, 0)),
            pl.BlockSpec((step_q, total_rows, R), lambda s: (s, 0, 0)),
        ],
        out_specs=pl.BlockSpec((total_rows, count * LAGS), lambda s: (0, 0)),
        scratch_shapes=[pltpu.VMEM((total_rows // 128, LAGS * count, 128), F32)],
        compiler_params=pltpu.CompilerParams(vmem_limit_bytes=40 * 2**20),
        name="correlate",
    )(exposure_per_row.reshape(1, total_rows), x, gathered)


def column_sums(mine, psum):
    kind = lax.broadcasted_iota(jnp.int32, (16, 256), 0)
    lane = lax.broadcasted_iota(jnp.int32, (16, 256), 1)
    pick = (lane // 16 == kind).astype(BF16)
    for j in range(Q // 16):
        part = mine[16 * j : 16 * (j + 1)].reshape(256, R)
        good = (part.astype(F32) > 0).astype(BF16)
        for i, what in enumerate((part, good)):
            psum[j // 4, i, 16 * (j % 4) : 16 * (j % 4 + 1), :] = lax.dot_general(
                pick, what, (((1,), (0,)), ((), ())), preferred_element_type=F32
            )


def row_scales(mine, means):
    zero = jnp.zeros((16, R), F32)

    def add(j, total):
        for i in range(16):
            flux = mine[16 * j + i].astype(F32)
            resid = jnp.where(flux > 0, flux - means[j, i : i + 1, :], 0.0)
            total = total + resid * resid
        return total

    total = lax.fori_loop(0, Q // 16, add, zero)
    return lax.rsqrt(jnp.sum(total, axis=1, keepdims=True) / PIX + 1e-06)


def diagonal():
    row = lax.broadcasted_iota(jnp.int32, (16, R), 0)
    lane = lax.broadcasted_iota(jnp.int32, (16, R), 1)
    return row == lane


def store_body(smooth, x, count):
    x[0, LAGS // 2 : LAGS // 2 + Q] = smooth[...].reshape(Q, count, R).astype(BF16)


def store_margins(x, tt):
    half = LAGS // 2
    count = x.shape[2]
    lane = lax.broadcasted_iota(jnp.int32, (half * count, R), 1)

    def rolled(first, shift, edge):
        part = x[tt, first : first + half].reshape(half * count, R).astype(F32)
        part = jnp.where(lane == edge, 0.0, pltpu.roll(part, shift, 1))
        return part.astype(BF16).reshape(half, count, R)

    x[tt, :half] = rolled(Q, 1, 0)
    x[tt, half + Q :] = rolled(half, R - 1, R - 1)


def cross_kernel(
    mine,
    index_ref,
    table_ref,
    templates_ref,
    out_ref,
    raw,
    ready,
    x,
    partner,
    psum,
    tsum,
    csum,
    rsum,
    means,
    row_scale,
    scale,
    bands,
    chunks,
    smooth,
    raw_send,
    raw_recv,
    x_sem,
    r_send,
    r_recv,
    t_sem,
    s_send,
    s_recv,
    m_send,
    m_recv,
    v_send,
    v_recv,
):
    me = lax.axis_index("blk")
    z, y, c = me // 4, (me // 2) % 2, me % 2
    planes = 4
    count = templates_ref.shape[0]
    span = Q // CHUNKS

    def blk(zz, yy, cc):
        return (zz * 2 + yy) * 2 + cc

    up, down = blk(z + 1, y, c), blk(z - 1, y, c)
    beside, twin = blk(z, 1 - y, c), blk(z, y, 1 - c)
    middle = (z == 1) | (z == 2)
    has_up, has_down = z < planes - 1, z > 0

    def remote(src, dst, send, recv, to):
        return pltpu.make_async_remote_copy(
            src_ref=src,
            dst_ref=dst,
            send_sem=send,
            recv_sem=recv,
            device_id={"blk": to},
            device_id_type=MESH,
        )

    barrier = pltpu.get_barrier_semaphore()

    def greet(o, _):
        pl.semaphore_signal(
            barrier, inc=1, device_id={"blk": lax.rem(me + o, 16)}, device_id_type=MESH
        )
        return 0

    lax.fori_loop(1, 16, greet, 0)
    raw[z, c] = mine[...]
    pl.semaphore_wait(barrier, 15)

    def raw_copy(zs, k, kind, to):
        part = raw.at[zs, c, pl.ds(k * span, span)]
        return remote(
            part, part, raw_send.at[kind, zs, k], raw_recv.at[zs * 2 + c, k], to
        )

    def from_twin(zs, k):
        part = raw.at[zs, 1 - c, pl.ds(k * span, span)]
        remote(
            part, part, raw_send.at[2, zs, k], raw_recv.at[zs * 2 + 1 - c, k], twin
        ).wait_recv()

    def on_sides(h, act):
        for sign in (1, -1):
            zs = z + sign * h
            pl.when((zs >= 0) & (zs < planes))(functools.partial(act, zs, sign))

    def send(s):
        h, k = s // CHUNKS, s % CHUNKS
        if h == 0:
            pl.when(has_up)(lambda: raw_copy(z, k, 0, up).start())
            pl.when(has_down)(lambda: raw_copy(z, k, 1, down).start())
            raw_copy(z, k, 2, twin).start()
        elif h < planes - 1:

            def onward(zs, sign):
                if sign > 0:
                    pl.when(has_down)(lambda: raw_copy(zs, k, 1, down).start())
                else:
                    pl.when(has_up)(lambda: raw_copy(zs, k, 0, up).start())

            on_sides(h, onward)

    def arrive(s):
        h, k = s // CHUNKS + 1, s % CHUNKS

        def land(zs, sign):
            raw_copy(zs, k, 2, twin).wait_recv()
            raw_copy(zs, k, 2, twin).start()

        on_sides(h, land)

    def step(s, lead):
        arrive(s)
        send(s + lead)

    send(0)
    send(1)

    column_sums(mine, psum)
    to_twin = remote(psum.at[1 - c], tsum, t_sem.at[0], t_sem.at[1], twin)
    to_twin.start()
    spread_templates(table_ref, templates_ref, bands, chunks)

    def owner(w):
        return blk(1 + w // 2, w % 2, c)

    def sum_copy(w):
        return remote(
            csum.at[w], rsum.at[z * 2 + y], s_send.at[w], s_recv.at[z * 2 + y], owner(w)
        )

    def sum_from(i):
        return remote(csum.at[0], rsum.at[i], s_send.at[0], s_recv.at[i], twin)

    def mean_copy(w, o):
        part = means.at[4 * c + w]
        chip = lax.rem(z * 2 + y + o, 8)
        return remote(
            part, part, m_send.at[o], m_recv.at[w], blk(chip // 2, chip % 2, c)
        )

    mine_w = (z - 1) * 2 + y

    def sums_to_owners():
        to_twin.wait_recv()
        for w in range(4):
            rows = slice(16 * w, 16 * (w + 1))
            csum[w] = psum[c, :, rows, :] + tsum[:, rows, :]
            away = jnp.logical_not(middle & (mine_w == w))
            pl.when(away)(lambda: sum_copy(w).start())

            @pl.when(jnp.logical_not(away))
            def _():
                rsum[z * 2 + y] = csum[w]

    def means_from_owner():
        @pl.when(middle)
        def _():
            for i in range(8):
                pl.when(z * 2 + y != i)(lambda: sum_from(i).wait_recv())
            total = rsum[0]
            for i in range(1, 8):
                total = total + rsum[i]
            means[4 * c + mine_w] = total[0] / jnp.maximum(total[1], 1.0)
            for o in range(1, 8):
                mean_copy(mine_w, o).start()

    half_means = remote(
        means.at[pl.ds(4 * c, 4)],
        means.at[pl.ds(4 * c, 4)],
        t_sem.at[2],
        t_sem.at[3],
        twin,
    )

    def means_to_twin():
        for w in range(4):
            away = jnp.logical_not(middle & (mine_w == w))
            pl.when(away)(lambda: mean_copy(w, 1).wait_recv())
        half_means.start()

    def scale_copy(o):
        at = lax.rem(z * 2 + c + o, 8)
        return remote(
            row_scale.at[z * 2 + c],
            row_scale.at[z * 2 + c],
            v_send.at[o],
            v_recv.at[z * 2 + c],
            blk(at // 2, y, at % 2),
        )

    def scales_out():
        half_means.wait_recv()
        own = row_scales(mine, means)
        row_scale[z * 2 + c] = jnp.sum(
            jnp.where(diagonal(), own, 0.0), axis=0, keepdims=True
        )
        for o in range(1, 8):
            scale_copy(o).start()

    def scales_in():
        for i in range(8):
            part = row_scale.at[i]
            pl.when(z * 2 + c != i)(
                lambda: remote(part, part, v_send.at[0], v_recv.at[i], twin).wait_recv()
            )
            column = jnp.sum(
                jnp.where(diagonal(), row_scale[i], 0.0), axis=1, keepdims=True
            )
            scale[i] = jnp.broadcast_to(column, (16, R))

    def x_copy(k):
        rows = pl.ds(LAGS // 2 + k * span, span)
        return remote(
            x.at[0, rows], x.at[1, rows], x_sem.at[0, k], x_sem.at[1, k], beside
        )

    smooth_templates(index_ref, bands, chunks, smooth, 0, 2, count)
    sums_to_owners()
    send(2)
    smooth_templates(index_ref, bands, chunks, smooth, 2, count, count)
    store_body(smooth, x, count)
    x_copy(0).start()
    for zs in range(planes):
        ready[zs, :AHEAD] = jnp.zeros((AHEAD, 32, R), BF16)
        ready[zs, AHEAD + Q :] = jnp.zeros((ready.shape[1] - AHEAD - Q, 32, R), BF16)
    store_margins(x, 0)
    after = {3: means_from_owner, 6: means_to_twin, 7: scales_out, 11: scales_in}
    for s in range(12):
        step(s, LEAD)
        if 0 < s + 1 < CHUNKS:
            x_copy(s + 1).start()
        after.get(s, lambda: None)()
    for s in range(12 + LEAD, 20):
        send(s)

    def normalise(zs, first, last):
        for cc in range(2):
            factor = scale[zs * 2 + cc]

            def tile(j, _):
                for i in range(16):
                    flux = raw[zs, cc, 16 * j + i].astype(F32)
                    resid = jnp.where(flux > 0, flux - means[j, i : i + 1, :], 0.0)
                    ready[zs, AHEAD + 16 * j + i, 16 * cc : 16 * (cc + 1), :] = (
                        resid * factor
                    ).astype(BF16)
                return 0

            lax.fori_loop(first, last, tile, 0)

    def product(zs, quarter):
        first = 32 * quarter
        width = 32 if quarter < 3 else 40
        right = jnp.concatenate(
            [ready[zs, first + i : first + i + 8].reshape(256, R) for i in range(width)],
            axis=1,
        )
        left = jnp.concatenate(
            [
                jnp.concatenate(
                    [x[tt, first + i + 8 * a] for tt in range(2) for a in range(8)], axis=0
                )
                for i in range(width)
            ],
            axis=1,
        )
        part = lax.dot_general(left, right, NT_DIMS, preferred_element_type=F32)
        if quarter == 0:
            out_ref[zs * 2 + y] = part[:128]
            partner[zs] = part[128:]
        else:
            out_ref[zs * 2 + y] += part[:128]
            partner[zs] += part[128:]

    def result_copy(zs):
        return remote(
            partner.at[zs], out_ref.at[zs * 2 + y], r_send.at[zs], r_recv.at[zs], beside
        )

    def slot(i):
        near = jnp.where(z < 2, z + 1, z - 1)
        far = jnp.where(z == 0, 2, jnp.where(z == 1, 0, jnp.where(z == 2, 3, 1)))
        end = jnp.where(z < 2, 3, 0)
        return jnp.where(
            i == 0, z, jnp.where(i == 1, near, jnp.where(i == 2, far, end))
        )

    def block(i, _):
        zs = slot(i)

        @pl.when(i == 0)
        def _():
            for k in range(CHUNKS):
                x_copy(k).wait_recv()
            store_margins(x, 1)

        @pl.when(i == 1)
        def _():
            for s in range(12, 14):
                step(s, 8)

        @pl.when(i == 2)
        def _():
            for s in range(14, 16):
                step(s, 8)

        @pl.when(i < 3)
        def _():
            for k in range(CHUNKS):
                from_twin(zs, k)
            normalise(zs, 0, Q // 16)

        for quarter in range(4):

            @pl.when(i == 3)
            def _():
                for s in range(16 + 2 * quarter, 18 + 2 * quarter):
                    arrive(s)
                for k in range(2 * quarter, 2 * quarter + 2):
                    from_twin(zs, k)
                normalise(zs, 2 * quarter, 2 * quarter + 2)

            pl.when(z < planes)(functools.partial(product, zs, quarter))
        result_copy(zs).start()
        return 0

    lax.fori_loop(0, planes, block, 0)

    for k in range(CHUNKS):
        x_copy(k).wait_send()
    to_twin.wait_send()
    half_means.wait_send()
    for w in range(4):
        away = jnp.logical_not(middle & (mine_w == w))
        pl.when(away)(lambda: sum_copy(w).wait_send())

    @pl.when(middle)
    def _():
        for o in range(1, 8):
            mean_copy(mine_w, o).wait_send()

    for o in range(1, 8):
        scale_copy(o).wait_send()

    def sent(k, _):
        for zs in range(planes):
            raw_copy(zs, k, 2, twin).wait_send()
            pl.when(has_up & (zs <= z))(lambda: raw_copy(zs, k, 0, up).wait_send())
            pl.when(has_down & (zs >= z))(lambda: raw_copy(zs, k, 1, down).wait_send())
        return 0

    lax.fori_loop(0, CHUNKS, sent, 0)
    for zs in range(planes):
        result_copy(zs).wait_send()
    for zs in range(planes):
        result_copy(zs).wait_recv()


def cross(masked, templates, template_kernel_index, line_spread_table):
    count = templates.shape[0]
    rows = masked.shape[1]
    vmem = pl.BlockSpec(memory_space=pltpu.VMEM)
    dma = pltpu.SemaphoreType.DMA
    return pl.pallas_call(
        cross_kernel,
        out_shape=jax.ShapeDtypeStruct((8, 8 * count, 256), F32),
        in_specs=[vmem, pl.BlockSpec(memory_space=pltpu.SMEM), vmem, vmem],
        out_specs=vmem,
        scratch_shapes=[
            pltpu.VMEM((4, 2, Q, rows, R), BF16),
            pltpu.VMEM((4, Q + 16, 2 * rows, R), BF16),
            pltpu.VMEM((2, Q + LAGS, count, R), BF16),
            pltpu.VMEM((4, 8 * count, 256), F32),
            pltpu.VMEM((2, 2, Q // 2, R), F32),
            pltpu.VMEM((2, Q // 2, R), F32),
            pltpu.VMEM((4, 2, 16, R), F32),
            pltpu.VMEM((8, 2, 16, R), F32),
            pltpu.VMEM((8, 16, R), F32),
            pltpu.VMEM((8, 1, R), F32),
            pltpu.VMEM((8, 16, R), F32),
            pltpu.VMEM((KERNELS, Q, 2 * BAND), BF16),
            pltpu.VMEM((BAND // 128, R * count, 128), F32),
            pltpu.VMEM((Q * count, R), F32),
            dma((3, 4, CHUNKS)),
            dma((8, CHUNKS)),
            dma((2, CHUNKS)),
            dma((4,)),
            dma((4,)),
            dma((4,)),
            dma((4,)),
            dma((8,)),
            dma((8,)),
            dma((4,)),
            dma((8,)),
            dma((8,)),
        ],
        compiler_params=pltpu.CompilerParams(
            collective_id=0, has_side_effects=True, vmem_limit_bytes=48 * 2**20
        ),
        name="cross",
    )(masked, template_kernel_index, line_spread_table, templates)


def place_kernel(rows_ref, part_ref, out_ref, split):
    count = part_ref.shape[1] // 8
    lane = lax.broadcasted_iota(jnp.int32, (8 * count, 128), 1) // 32
    for h in range(2):
        for b in range(8):
            at = 7 - b
            piece = None
            for i in range(4):
                one = part_ref[4 * h + i, :, 128 * (at // 4) : 128 * (at // 4 + 1)]
                shift = 32 * (i - at % 4) % 128
                one = pltpu.roll(one, shift, 1) if shift else one
                piece = one if piece is None else jnp.where(lane == i, one, piece)
            for a in range(8):
                split[h, (8 * a + b) * count : (8 * a + b + 1) * count, :] = piece[
                    a * count : (a + 1) * count
                ]
    place_rows(rows_ref, split, out_ref, count)


def place(parts, exposure_per_row):
    total_rows = 32 * parts.shape[0]
    across = parts.shape[1] * 8
    return pl.pallas_call(
        place_kernel,
        out_shape=jax.ShapeDtypeStruct((total_rows, across), F32),
        in_specs=[pl.BlockSpec(memory_space=pltpu.VMEM)] * 2,
        out_specs=pl.BlockSpec(memory_space=pltpu.VMEM),
        scratch_shapes=[pltpu.VMEM((total_rows // 128, across, 128), F32)],
        compiler_params=pltpu.CompilerParams(vmem_limit_bytes=16 * 2**20),
        name="place",
    )(exposure_per_row.reshape(1, total_rows), parts)


def shards(
    devices,
    observed,
    good_pixel_mask,
    templates,
    template_kernel_index,
    line_spread_table,
    exposure_per_row,
):
    rows = observed.shape[0]
    flux = jnp.where(good_pixel_mask > 0, observed, 0)
    if devices == 16 and rows == 16 and templates.shape[0] == 16:
        masked = flux.reshape(rows, R, Q).transpose(2, 0, 1)
        parts = cross(masked, templates, template_kernel_index, line_spread_table)
        return place(parts, exposure_per_row)
    flux = flux.astype(F32)
    present = (flux > 0).astype(F32)
    sums, counts = jnp.sum(flux, axis=0), jnp.sum(present, axis=0)
    x = shape_templates(templates, template_kernel_index, line_spread_table)
    sums = lax.psum(jnp.stack([sums, counts]), "blk")
    mean = sums[0] / jnp.maximum(sums[1], 1.0)
    resid = present * (flux - mean[None, :])
    scale = lax.rsqrt(jnp.sum(resid * resid, axis=1) / PIX + 1e-06)
    ready = (resid * scale[:, None]).astype(BF16)
    ready = ready.reshape(rows, R, Q).transpose(2, 0, 1)
    gathered = lax.all_gather(ready, "blk", axis=1, tiled=True)
    return correlate(x, gathered, exposure_per_row)


def solution(mesh):
    in_specs = (
        P(("grp", "blk"), None),
        P(("grp", "blk"), None),
        P(("grp", "blk"), None),
        P(("grp", "blk")),
        P(),
        P("grp"),
    )
    out_specs = P("grp", "blk")
    return jax.shard_map(
        functools.partial(shards, mesh.shape["blk"]),
        mesh=mesh,
        in_specs=in_specs,
        out_specs=out_specs,
        check_vma=False,
    )
```

```python
import functools
import math

import jax
import jax.numpy as jnp
from jax import lax
from jax.experimental import pallas as pl
from jax.experimental.pallas import tpu as pltpu
from jax.sharding import PartitionSpec as P

PIX = 16384
LAGS = 64
TAPS = 97
KERNELS = 8
Q = 128
R = PIX // Q
BAND = 640
CHUNKS = 8
LEAD = 4
AHEAD = 7
PIECES = ((0, 4), (4, 7), (7, 8))
F32 = jnp.float32
BF16 = jnp.bfloat16
MESH = pl.DeviceIdType.MESH
NT_DIMS = (((1,), (1,)), ((), ()))


def template_kernel(index_ref, table_ref, templates_ref, x_ref, bands, chunks, smooth):
    count = templates_ref.shape[0]
    spread_templates(table_ref, templates_ref, bands, chunks)
    smooth_templates(index_ref, bands, chunks, smooth, 0, count, count)
    pack_templates(smooth, x_ref, count)


def spread_templates(table_ref, templates_ref, bands, chunks):
    count = templates_ref.shape[0]
    for k in range(KERNELS):
        row = jnp.concatenate(
            [table_ref[k : k + 1, :], jnp.zeros((1, BAND - TAPS), F32)], axis=1
        )
        row = jnp.broadcast_to(row, (Q, BAND))
        band = pltpu.roll(row, 0, 1, stride=4, stride_axis=0)
        high = band.astype(BF16)
        bands[k, :, :BAND] = high
        bands[k, :, BAND:] = (band - high.astype(F32)).astype(BF16)

    def spread(r, _):
        at = pl.multiple_of(r * (4 * Q), 128)
        piece = templates_ref[:, pl.ds(at, BAND)].astype(F32)
        for i in range(BAND // 128):
            chunks[i, pl.ds(pl.multiple_of(r * count, count), count), :] = piece[
                :, 128 * i : 128 * (i + 1)
            ]
        return 0

    lax.fori_loop(0, R - 1, spread, 0, unroll=8)
    last = (R - 1) * 4 * Q
    left = templates_ref.shape[1] - last
    tail = templates_ref[:, last:].astype(F32)
    tail = jnp.concatenate([tail, jnp.zeros((count, BAND - left), F32)], axis=1)
    for i in range(BAND // 128):
        chunks[i, (R - 1) * count :, :] = tail[:, 128 * i : 128 * (i + 1)]


def smooth_templates(index_ref, bands, chunks, smooth, first, last, count):
    for t in range(first, last):
        rows = [
            chunks[i, pl.ds(t, R, stride=count), :].astype(BF16) for i in range(BAND // 128)
        ]
        rows = jnp.concatenate(rows + rows, axis=1)
        flux = lax.dot_general(
            bands[index_ref[t]], rows, NT_DIMS, preferred_element_type=F32
        )
        total = jnp.sum(flux * flux)
        smooth[pl.ds(t, Q, stride=count), :] = flux * lax.rsqrt(
            jnp.full((1, 1), total) / PIX + 1e-06
        )


def pack_templates(smooth, x_ref, count):
    half = LAGS // 2
    body = smooth[...]
    lane = lax.broadcasted_iota(jnp.int32, (half * count, R), 1)
    x_ref[half * count : (half + Q) * count, :] = body.astype(BF16)
    before = pltpu.roll(body[(Q - half) * count :, :], 1, 1)
    x_ref[: half * count, :] = jnp.where(lane == 0, 0.0, before).astype(BF16)
    after = pltpu.roll(body[: half * count, :], R - 1, 1)
    x_ref[(half + Q) * count :, :] = jnp.where(lane == R - 1, 0.0, after).astype(BF16)


def shape_templates(templates, template_kernel_index, line_spread_table):
    count = templates.shape[0]
    return pl.pallas_call(
        template_kernel,
        out_shape=jax.ShapeDtypeStruct(((Q + LAGS) * count, R), BF16),
        in_specs=[
            pl.BlockSpec(memory_space=pltpu.SMEM),
            pl.BlockSpec(memory_space=pltpu.VMEM),
            pl.BlockSpec(memory_space=pltpu.VMEM),
        ],
        out_specs=pl.BlockSpec(memory_space=pltpu.VMEM),
        scratch_shapes=[
            pltpu.VMEM((KERNELS, Q, 2 * BAND), BF16),
            pltpu.VMEM((BAND // 128, R * count, 128), F32),
            pltpu.VMEM((Q * count, R), F32),
        ],
        compiler_params=pltpu.CompilerParams(vmem_limit_bytes=40 * 2**20),
        cost_estimate=pl.CostEstimate(
            flops=2 * count * Q * R * 2 * BAND, bytes_accessed=6 * 2**20, transcendentals=0
        ),
        name="shape_templates",
    )(template_kernel_index, line_spread_table, templates)


def place_rows(rows_ref, acc, out_ref, count):
    total_rows = rows_ref.shape[1]
    chosen = (
        lax.broadcasted_iota(jnp.int32, (total_rows, total_rows), 0) == rows_ref[...]
    ).astype(BF16)
    both = jnp.concatenate([chosen, chosen], axis=1)
    for t in range(0, count, 2):
        part = jnp.concatenate(
            [
                jnp.concatenate(
                    [
                        acc[h, pl.ds(t + i, LAGS, stride=count), :]
                        for h in range(total_rows // 128)
                    ],
                    axis=1,
                )
                for i in range(2)
            ],
            axis=0,
        ) * F32(1.0 / math.sqrt(PIX))
        high = part.astype(BF16)
        low = (part - high.astype(F32)).astype(BF16)
        out_ref[:, t * LAGS : (t + 2) * LAGS] = lax.dot_general(
            both,
            jnp.concatenate([high, low], axis=1),
            NT_DIMS,
            preferred_element_type=F32,
        )


def correlate_kernel(step_q, rows_ref, x_ref, g_ref, out_ref, acc):
    step = pl.program_id(0)
    total_rows = rows_ref.shape[1]
    count = x_ref.shape[0] // (Q + LAGS)
    tile = 256

    @pl.when(step == 0)
    def _():
        acc[...] = jnp.zeros_like(acc)

    right = jnp.concatenate([g_ref[i] for i in range(step_q)], axis=1)
    for m in range(LAGS * count // tile):
        left = jnp.concatenate(
            [
                x_ref[pl.ds(pl.multiple_of((step * step_q + i) * count + m * tile, 16), tile), :]
                for i in range(step_q)
            ],
            axis=1,
        )
        part = lax.dot_general(left, right, NT_DIMS, preferred_element_type=F32)
        for h in range(total_rows // 128):
            acc[h, m * tile : (m + 1) * tile, :] += part[:, 128 * h : 128 * (h + 1)]

    @pl.when(step == pl.num_programs(0) - 1)
    def _():
        place_rows(rows_ref, acc, out_ref, count)


def correlate(x, gathered, exposure_per_row):
    total_rows = gathered.shape[1]
    count = x.shape[0] // (Q + LAGS)
    step_q = 8
    return pl.pallas_call(
        functools.partial(correlate_kernel, step_q),
        grid=(Q // step_q,),
        out_shape=jax.ShapeDtypeStruct((total_rows, count * LAGS), F32),
        in_specs=[
            pl.BlockSpec((1, total_rows), lambda s: (0, 0)),
            pl.BlockSpec(x.shape, lambda s: (0, 0)),
            pl.BlockSpec((step_q, total_rows, R), lambda s: (s, 0, 0)),
        ],
        out_specs=pl.BlockSpec((total_rows, count * LAGS), lambda s: (0, 0)),
        scratch_shapes=[pltpu.VMEM((total_rows // 128, LAGS * count, 128), F32)],
        compiler_params=pltpu.CompilerParams(vmem_limit_bytes=40 * 2**20),
        name="correlate",
    )(exposure_per_row.reshape(1, total_rows), x, gathered)


def column_sums(mine, psum):
    kind = lax.broadcasted_iota(jnp.int32, (16, 256), 0)
    lane = lax.broadcasted_iota(jnp.int32, (16, 256), 1)
    pick = (lane // 16 == kind).astype(BF16)
    for j in range(Q // 16):
        part = mine[16 * j : 16 * (j + 1)].reshape(256, R)
        good = (part.astype(F32) > 0).astype(BF16)
        for i, what in enumerate((part, good)):
            psum[j // 4, i, 16 * (j % 4) : 16 * (j % 4 + 1), :] = lax.dot_general(
                pick, what, (((1,), (0,)), ((), ())), preferred_element_type=F32
            )


def row_scales(mine, means):
    zero = jnp.zeros((16, R), F32)

    def add(j, total):
        for i in range(16):
            flux = mine[16 * j + i].astype(F32)
            resid = jnp.where(flux > 0, flux - means[j, i : i + 1, :], 0.0)
            total = total + resid * resid
        return total

    total = lax.fori_loop(0, Q // 16, add, zero)
    return lax.rsqrt(jnp.sum(total, axis=1, keepdims=True) / PIX + 1e-06)


def diagonal():
    row = lax.broadcasted_iota(jnp.int32, (16, R), 0)
    lane = lax.broadcasted_iota(jnp.int32, (16, R), 1)
    return row == lane


def store_body(smooth, x, count):
    x[0, LAGS // 2 : LAGS // 2 + Q] = smooth[...].reshape(Q, count, R).astype(BF16)


def store_margins(x, tt):
    half = LAGS // 2
    count = x.shape[2]
    lane = lax.broadcasted_iota(jnp.int32, (half * count, R), 1)

    def rolled(first, shift, edge):
        part = x[tt, first : first + half].reshape(half * count, R).astype(F32)
        part = jnp.where(lane == edge, 0.0, pltpu.roll(part, shift, 1))
        return part.astype(BF16).reshape(half, count, R)

    x[tt, :half] = rolled(Q, 1, 0)
    x[tt, half + Q :] = rolled(half, R - 1, R - 1)


def cross_kernel(
    mine,
    index_ref,
    table_ref,
    templates_ref,
    out_ref,
    raw,
    ready,
    x,
    partner,
    psum,
    tsum,
    csum,
    rsum,
    means,
    row_scale,
    scale,
    bands,
    chunks,
    smooth,
    raw_send,
    raw_recv,
    x_sem,
    r_send,
    r_recv,
    t_sem,
    s_send,
    s_recv,
    m_send,
    m_recv,
    v_send,
    v_recv,
    tail,
    tail_sem,
):
    me = lax.axis_index("blk")
    z, y, c = me // 4, (me // 2) % 2, me % 2
    planes = 4
    count = templates_ref.shape[0]
    span = Q // CHUNKS

    def blk(zz, yy, cc):
        return (zz * 2 + yy) * 2 + cc

    up, down = blk(z + 1, y, c), blk(z - 1, y, c)
    beside, twin = blk(z, 1 - y, c), blk(z, y, 1 - c)
    middle = (z == 1) | (z == 2)
    has_up, has_down = z < planes - 1, z > 0

    def remote(src, dst, send, recv, to):
        return pltpu.make_async_remote_copy(
            src_ref=src,
            dst_ref=dst,
            send_sem=send,
            recv_sem=recv,
            device_id={"blk": to},
            device_id_type=MESH,
        )

    barrier = pltpu.get_barrier_semaphore()

    def greet(o, _):
        pl.semaphore_signal(
            barrier, inc=1, device_id={"blk": lax.rem(me + o, 16)}, device_id_type=MESH
        )
        return 0

    lax.fori_loop(1, 16, greet, 0)
    raw[z, c] = mine[...]
    pl.semaphore_wait(barrier, 15)

    def raw_copy(zs, k, kind, to):
        part = raw.at[zs, c, pl.ds(k * span, span)]
        return remote(
            part, part, raw_send.at[kind, zs, k], raw_recv.at[zs * 2 + c, k], to
        )

    def from_twin(zs, k):
        part = raw.at[zs, 1 - c, pl.ds(k * span, span)]
        remote(
            part, part, raw_send.at[2, zs, k], raw_recv.at[zs * 2 + 1 - c, k], twin
        ).wait_recv()

    def on_sides(h, act):
        for sign in (1, -1):
            zs = z + sign * h
            pl.when((zs >= 0) & (zs < planes))(functools.partial(act, zs, sign))

    def send(s):
        h, k = s // CHUNKS, s % CHUNKS
        if h == 0:
            pl.when(has_up)(lambda: raw_copy(z, k, 0, up).start())
            pl.when(has_down)(lambda: raw_copy(z, k, 1, down).start())
            raw_copy(z, k, 2, twin).start()
        elif h < planes - 1:

            def onward(zs, sign):
                if sign > 0:
                    pl.when(has_down)(lambda: raw_copy(zs, k, 1, down).start())
                else:
                    pl.when(has_up)(lambda: raw_copy(zs, k, 0, up).start())

            on_sides(h, onward)

    def arrive(s):
        h, k = s // CHUNKS + 1, s % CHUNKS

        def land(zs, sign):
            raw_copy(zs, k, 2, twin).wait_recv()
            raw_copy(zs, k, 2, twin).start()

        on_sides(h, land)

    def step(s, lead):
        arrive(s)
        send(s + lead)

    send(0)
    send(1)

    column_sums(mine, psum)
    to_twin = remote(psum.at[1 - c], tsum, t_sem.at[0], t_sem.at[1], twin)
    to_twin.start()
    spread_templates(table_ref, templates_ref, bands, chunks)

    def owner(w):
        return blk(1 + w // 2, w % 2, c)

    def sum_copy(w):
        return remote(
            csum.at[w], rsum.at[z * 2 + y], s_send.at[w], s_recv.at[z * 2 + y], owner(w)
        )

    def sum_from(i):
        return remote(csum.at[0], rsum.at[i], s_send.at[0], s_recv.at[i], twin)

    def mean_copy(w, o):
        part = means.at[4 * c + w]
        chip = lax.rem(z * 2 + y + o, 8)
        return remote(
            part, part, m_send.at[o], m_recv.at[w], blk(chip // 2, chip % 2, c)
        )

    mine_w = (z - 1) * 2 + y

    def sums_to_owners():
        to_twin.wait_recv()
        for w in range(4):
            rows = slice(16 * w, 16 * (w + 1))
            csum[w] = psum[c, :, rows, :] + tsum[:, rows, :]
            away = jnp.logical_not(middle & (mine_w == w))
            pl.when(away)(lambda: sum_copy(w).start())

            @pl.when(jnp.logical_not(away))
            def _():
                rsum[z * 2 + y] = csum[w]

    def means_from_owner():
        @pl.when(middle)
        def _():
            for i in range(8):
                pl.when(z * 2 + y != i)(lambda: sum_from(i).wait_recv())
            total = rsum[0]
            for i in range(1, 8):
                total = total + rsum[i]
            means[4 * c + mine_w] = total[0] / jnp.maximum(total[1], 1.0)
            for o in range(1, 8):
                mean_copy(mine_w, o).start()

    half_means = remote(
        means.at[pl.ds(4 * c, 4)],
        means.at[pl.ds(4 * c, 4)],
        t_sem.at[2],
        t_sem.at[3],
        twin,
    )

    def means_to_twin():
        for w in range(4):
            away = jnp.logical_not(middle & (mine_w == w))
            pl.when(away)(lambda: mean_copy(w, 1).wait_recv())
        half_means.start()

    def scale_copy(o):
        at = lax.rem(z * 2 + c + o, 8)
        return remote(
            row_scale.at[z * 2 + c],
            row_scale.at[z * 2 + c],
            v_send.at[o],
            v_recv.at[z * 2 + c],
            blk(at // 2, y, at % 2),
        )

    def scales_out():
        half_means.wait_recv()
        own = row_scales(mine, means)
        row_scale[z * 2 + c] = jnp.sum(
            jnp.where(diagonal(), own, 0.0), axis=0, keepdims=True
        )
        for o in range(1, 8):
            scale_copy(o).start()

    def scales_in():
        for i in range(8):
            part = row_scale.at[i]
            pl.when(z * 2 + c != i)(
                lambda: remote(part, part, v_send.at[0], v_recv.at[i], twin).wait_recv()
            )
            column = jnp.sum(
                jnp.where(diagonal(), row_scale[i], 0.0), axis=1, keepdims=True
            )
            scale[i] = jnp.broadcast_to(column, (16, R))

    def x_copy(k):
        rows = pl.ds(LAGS // 2 + k * span, span)
        return remote(
            x.at[0, rows], x.at[1, rows], x_sem.at[0, k], x_sem.at[1, k], beside
        )

    smooth_templates(index_ref, bands, chunks, smooth, 0, 2, count)
    sums_to_owners()
    send(2)
    send(3)
    smooth_templates(index_ref, bands, chunks, smooth, 2, count, count)
    store_body(smooth, x, count)
    x_copy(0).start()
    for zs in range(planes):
        ready[zs, :AHEAD] = jnp.zeros((AHEAD, 32, R), BF16)
        ready[zs, AHEAD + Q :] = jnp.zeros((ready.shape[1] - AHEAD - Q, 32, R), BF16)
    store_margins(x, 0)
    after = {2: means_from_owner, 5: means_to_twin, 6: scales_out, 9: scales_in}
    for s in range(10):
        step(s, LEAD)
        if 0 < s + 1 < CHUNKS:
            x_copy(s + 1).start()
        after.get(s, lambda: None)()
    for s in range(10 + LEAD, 18):
        send(s)

    def normalise(zs, first, last):
        for cc in range(2):
            factor = scale[zs * 2 + cc]

            def tile(j, _):
                for i in range(16):
                    flux = raw[zs, cc, 16 * j + i].astype(F32)
                    resid = jnp.where(flux > 0, flux - means[j, i : i + 1, :], 0.0)
                    ready[zs, AHEAD + 16 * j + i, 16 * cc : 16 * (cc + 1), :] = (
                        resid * factor
                    ).astype(BF16)
                return 0

            lax.fori_loop(first, last, tile, 0)

    def product(zs, first, last, ends=False):
        right = jnp.concatenate(
            [ready[zs, i : i + 8].reshape(256, R) for i in range(first, last)], axis=1
        )
        left = jnp.concatenate(
            [
                jnp.concatenate(
                    [x[tt, i + 8 * a] for tt in range(2) for a in range(8)], axis=0
                )
                for i in range(first, last)
            ],
            axis=1,
        )
        part = lax.dot_general(left, right, NT_DIMS, preferred_element_type=F32)
        if ends:
            out_ref[zs * 2 + y] += part[:128]
            tail[0] = part[128:].astype(BF16)
        elif first == 0:
            out_ref[zs * 2 + y] = part[:128]
            partner[zs] = part[128:]
        else:
            out_ref[zs * 2 + y] += part[:128]
            partner[zs] += part[128:]

    def result_copy(zs):
        return remote(
            partner.at[zs], out_ref.at[zs * 2 + y], r_send.at[zs], r_recv.at[zs], beside
        )

    def slot(i):
        near = jnp.where(z < 2, z + 1, z - 1)
        far = jnp.where(z == 0, 2, jnp.where(z == 1, 0, jnp.where(z == 2, 3, 1)))
        end = jnp.where(z < 2, 3, 0)
        return jnp.where(
            i == 0, z, jnp.where(i == 1, near, jnp.where(i == 2, far, end))
        )

    def block(i, _):
        zs = slot(i)

        @pl.when(i == 0)
        def _():
            for k in range(CHUNKS):
                x_copy(k).wait_recv()
            store_margins(x, 1)

        @pl.when(i == 1)
        def _():
            for s in range(10, 14):
                step(s, 8)

        @pl.when(i == 2)
        def _():
            for s in range(14, 16):
                step(s, 8)

        for k in range(CHUNKS):
            from_twin(zs, k)
        normalise(zs, 0, Q // 16)

        @pl.when(z < planes)
        def _():
            for quarter in range(4):
                product(zs, 32 * quarter, 32 * quarter + (32 if quarter < 3 else 40))

        result_copy(zs).start()
        return 0

    lax.fori_loop(0, 3, block, 0)
    last = slot(3)
    for first, end in PIECES:
        for k in range(first, end):
            arrive(16 + k)
        for k in range(first, end):
            from_twin(last, k)
        normalise(last, first, end)
        ends = end == CHUNKS
        low, high = span * first, span * end + (8 if ends else 0)
        pl.when(z < planes)(functools.partial(product, last, low, high, ends))
        if first == PIECES[-2][0]:
            result_copy(last).start()
    tail_copy = remote(tail.at[0], tail.at[1], tail_sem.at[0], tail_sem.at[1], beside)
    tail_copy.start()

    for k in range(CHUNKS):
        x_copy(k).wait_send()
    to_twin.wait_send()
    half_means.wait_send()
    for w in range(4):
        away = jnp.logical_not(middle & (mine_w == w))
        pl.when(away)(lambda: sum_copy(w).wait_send())

    @pl.when(middle)
    def _():
        for o in range(1, 8):
            mean_copy(mine_w, o).wait_send()

    for o in range(1, 8):
        scale_copy(o).wait_send()

    def sent(k, _):
        for zs in range(planes):
            raw_copy(zs, k, 2, twin).wait_send()
            pl.when(has_up & (zs <= z))(lambda: raw_copy(zs, k, 0, up).wait_send())
            pl.when(has_down & (zs >= z))(lambda: raw_copy(zs, k, 1, down).wait_send())
        return 0

    lax.fori_loop(0, CHUNKS, sent, 0)
    for zs in range(planes):
        result_copy(zs).wait_send()
    tail_copy.wait_send()
    for zs in range(planes):
        result_copy(zs).wait_recv()
    tail_copy.wait_recv()
    out_ref[last * 2 + 1 - y] += tail[1].astype(F32)


def cross(masked, templates, template_kernel_index, line_spread_table):
    count = templates.shape[0]
    rows = masked.shape[1]
    vmem = pl.BlockSpec(memory_space=pltpu.VMEM)
    dma = pltpu.SemaphoreType.DMA
    return pl.pallas_call(
        cross_kernel,
        out_shape=jax.ShapeDtypeStruct((8, 8 * count, 256), F32),
        in_specs=[vmem, pl.BlockSpec(memory_space=pltpu.SMEM), vmem, vmem],
        out_specs=vmem,
        scratch_shapes=[
            pltpu.VMEM((4, 2, Q, rows, R), BF16),
            pltpu.VMEM((4, Q + 16, 2 * rows, R), BF16),
            pltpu.VMEM((2, Q + LAGS, count, R), BF16),
            pltpu.VMEM((4, 8 * count, 256), F32),
            pltpu.VMEM((2, 2, Q // 2, R), F32),
            pltpu.VMEM((2, Q // 2, R), F32),
            pltpu.VMEM((4, 2, 16, R), F32),
            pltpu.VMEM((8, 2, 16, R), F32),
            pltpu.VMEM((8, 16, R), F32),
            pltpu.VMEM((8, 1, R), F32),
            pltpu.VMEM((8, 16, R), F32),
            pltpu.VMEM((KERNELS, Q, 2 * BAND), BF16),
            pltpu.VMEM((BAND // 128, R * count, 128), F32),
            pltpu.VMEM((Q * count, R), F32),
            dma((3, 4, CHUNKS)),
            dma((8, CHUNKS)),
            dma((2, CHUNKS)),
            dma((4,)),
            dma((4,)),
            dma((4,)),
            dma((4,)),
            dma((8,)),
            dma((8,)),
            dma((4,)),
            dma((8,)),
            dma((8,)),
            pltpu.VMEM((2, 8 * count, 256), BF16),
            dma((2,)),
        ],
        compiler_params=pltpu.CompilerParams(
            collective_id=0, has_side_effects=True, vmem_limit_bytes=48 * 2**20
        ),
        name="cross",
    )(masked, template_kernel_index, line_spread_table, templates)


def place_kernel(rows_ref, part_ref, out_ref, split):
    count = part_ref.shape[1] // 8
    lane = lax.broadcasted_iota(jnp.int32, (8 * count, 128), 1) // 32
    for h in range(2):
        for b in range(8):
            at = 7 - b
            piece = None
            for i in range(4):
                one = part_ref[4 * h + i, :, 128 * (at // 4) : 128 * (at // 4 + 1)]
                shift = 32 * (i - at % 4) % 128
                one = pltpu.roll(one, shift, 1) if shift else one
                piece = one if piece is None else jnp.where(lane == i, one, piece)
            for a in range(8):
                split[h, (8 * a + b) * count : (8 * a + b + 1) * count, :] = piece[
                    a * count : (a + 1) * count
                ]
    place_rows(rows_ref, split, out_ref, count)


def place(parts, exposure_per_row):
    total_rows = 32 * parts.shape[0]
    across = parts.shape[1] * 8
    return pl.pallas_call(
        place_kernel,
        out_shape=jax.ShapeDtypeStruct((total_rows, across), F32),
        in_specs=[pl.BlockSpec(memory_space=pltpu.VMEM)] * 2,
        out_specs=pl.BlockSpec(memory_space=pltpu.VMEM),
        scratch_shapes=[pltpu.VMEM((total_rows // 128, across, 128), F32)],
        compiler_params=pltpu.CompilerParams(vmem_limit_bytes=16 * 2**20),
        name="place",
    )(exposure_per_row.reshape(1, total_rows), parts)


def shards(
    devices,
    observed,
    good_pixel_mask,
    templates,
    template_kernel_index,
    line_spread_table,
    exposure_per_row,
):
    rows = observed.shape[0]
    flux = jnp.where(good_pixel_mask > 0, observed, 0)
    if devices == 16 and rows == 16 and templates.shape[0] == 16:
        masked = flux.reshape(rows, R, Q).transpose(2, 0, 1)
        parts = cross(masked, templates, template_kernel_index, line_spread_table)
        return place(parts, exposure_per_row)
    flux = flux.astype(F32)
    present = (flux > 0).astype(F32)
    sums, counts = jnp.sum(flux, axis=0), jnp.sum(present, axis=0)
    x = shape_templates(templates, template_kernel_index, line_spread_table)
    sums = lax.psum(jnp.stack([sums, counts]), "blk")
    mean = sums[0] / jnp.maximum(sums[1], 1.0)
    resid = present * (flux - mean[None, :])
    scale = lax.rsqrt(jnp.sum(resid * resid, axis=1) / PIX + 1e-06)
    ready = (resid * scale[:, None]).astype(BF16)
    ready = ready.reshape(rows, R, Q).transpose(2, 0, 1)
    gathered = lax.all_gather(ready, "blk", axis=1, tiled=True)
    return correlate(x, gathered, exposure_per_row)


def solution(mesh):
    in_specs = (
        P(("grp", "blk"), None),
        P(("grp", "blk"), None),
        P(("grp", "blk"), None),
        P(("grp", "blk")),
        P(),
        P("grp"),
    )
    out_specs = P("grp", "blk")
    return jax.shard_map(
        functools.partial(shards, mesh.shape["blk"]),
        mesh=mesh,
        in_specs=in_specs,
        out_specs=out_specs,
        check_vma=False,
    )
```

```python
import functools
import math

import jax
import jax.numpy as jnp
from jax import lax
from jax.experimental import pallas as pl
from jax.experimental.pallas import tpu as pltpu
from jax.sharding import PartitionSpec as P

PIX = 16384
LAGS = 64
TAPS = 97
KERNELS = 8
Q = 128
R = PIX // Q
BAND = 640
CHUNKS = 8
LEAD = 4
AHEAD = 7
PIECES = ((0, 4), (4, 6), (6, 8))
F32 = jnp.float32
BF16 = jnp.bfloat16
MESH = pl.DeviceIdType.MESH
NT_DIMS = (((1,), (1,)), ((), ()))


def template_kernel(index_ref, table_ref, templates_ref, x_ref, bands, chunks, smooth):
    count = templates_ref.shape[0]
    spread_templates(table_ref, templates_ref, bands, chunks)
    smooth_templates(index_ref, bands, chunks, smooth, 0, count, count)
    pack_templates(smooth, x_ref, count)


def spread_templates(table_ref, templates_ref, bands, chunks):
    count = templates_ref.shape[0]
    for k in range(KERNELS):
        row = jnp.concatenate(
            [table_ref[k : k + 1, :], jnp.zeros((1, BAND - TAPS), F32)], axis=1
        )
        row = jnp.broadcast_to(row, (Q, BAND))
        band = pltpu.roll(row, 0, 1, stride=4, stride_axis=0)
        high = band.astype(BF16)
        bands[k, :, :BAND] = high
        bands[k, :, BAND:] = (band - high.astype(F32)).astype(BF16)

    def spread(r, _):
        at = pl.multiple_of(r * (4 * Q), 128)
        piece = templates_ref[:, pl.ds(at, BAND)].astype(F32)
        for i in range(BAND // 128):
            chunks[i, pl.ds(pl.multiple_of(r * count, count), count), :] = piece[
                :, 128 * i : 128 * (i + 1)
            ]
        return 0

    lax.fori_loop(0, R - 1, spread, 0, unroll=8)
    last = (R - 1) * 4 * Q
    left = templates_ref.shape[1] - last
    tail = templates_ref[:, last:].astype(F32)
    tail = jnp.concatenate([tail, jnp.zeros((count, BAND - left), F32)], axis=1)
    for i in range(BAND // 128):
        chunks[i, (R - 1) * count :, :] = tail[:, 128 * i : 128 * (i + 1)]


def smooth_templates(index_ref, bands, chunks, smooth, first, last, count):
    for t in range(first, last):
        rows = [
            chunks[i, pl.ds(t, R, stride=count), :].astype(BF16) for i in range(BAND // 128)
        ]
        rows = jnp.concatenate(rows + rows, axis=1)
        flux = lax.dot_general(
            bands[index_ref[t]], rows, NT_DIMS, preferred_element_type=F32
        )
        total = jnp.sum(flux * flux)
        smooth[pl.ds(t, Q, stride=count), :] = flux * lax.rsqrt(
            jnp.full((1, 1), total) / PIX + 1e-06
        )


def pack_templates(smooth, x_ref, count):
    half = LAGS // 2
    body = smooth[...]
    lane = lax.broadcasted_iota(jnp.int32, (half * count, R), 1)
    x_ref[half * count : (half + Q) * count, :] = body.astype(BF16)
    before = pltpu.roll(body[(Q - half) * count :, :], 1, 1)
    x_ref[: half * count, :] = jnp.where(lane == 0, 0.0, before).astype(BF16)
    after = pltpu.roll(body[: half * count, :], R - 1, 1)
    x_ref[(half + Q) * count :, :] = jnp.where(lane == R - 1, 0.0, after).astype(BF16)


def shape_templates(templates, template_kernel_index, line_spread_table):
    count = templates.shape[0]
    return pl.pallas_call(
        template_kernel,
        out_shape=jax.ShapeDtypeStruct(((Q + LAGS) * count, R), BF16),
        in_specs=[
            pl.BlockSpec(memory_space=pltpu.SMEM),
            pl.BlockSpec(memory_space=pltpu.VMEM),
            pl.BlockSpec(memory_space=pltpu.VMEM),
        ],
        out_specs=pl.BlockSpec(memory_space=pltpu.VMEM),
        scratch_shapes=[
            pltpu.VMEM((KERNELS, Q, 2 * BAND), BF16),
            pltpu.VMEM((BAND // 128, R * count, 128), F32),
            pltpu.VMEM((Q * count, R), F32),
        ],
        compiler_params=pltpu.CompilerParams(vmem_limit_bytes=40 * 2**20),
        cost_estimate=pl.CostEstimate(
            flops=2 * count * Q * R * 2 * BAND, bytes_accessed=6 * 2**20, transcendentals=0
        ),
        name="shape_templates",
    )(template_kernel_index, line_spread_table, templates)


def place_rows(rows_ref, acc, out_ref, count):
    total_rows = rows_ref.shape[1]
    chosen = (
        lax.broadcasted_iota(jnp.int32, (total_rows, total_rows), 0) == rows_ref[...]
    ).astype(BF16)
    both = jnp.concatenate([chosen, chosen], axis=1)
    for t in range(0, count, 2):
        part = jnp.concatenate(
            [
                jnp.concatenate(
                    [
                        acc[h, pl.ds(t + i, LAGS, stride=count), :]
                        for h in range(total_rows // 128)
                    ],
                    axis=1,
                )
                for i in range(2)
            ],
            axis=0,
        ) * F32(1.0 / math.sqrt(PIX))
        high = part.astype(BF16)
        low = (part - high.astype(F32)).astype(BF16)
        out_ref[:, t * LAGS : (t + 2) * LAGS] = lax.dot_general(
            both,
            jnp.concatenate([high, low], axis=1),
            NT_DIMS,
            preferred_element_type=F32,
        )


def correlate_kernel(step_q, rows_ref, x_ref, g_ref, out_ref, acc):
    step = pl.program_id(0)
    total_rows = rows_ref.shape[1]
    count = x_ref.shape[0] // (Q + LAGS)
    tile = 256

    @pl.when(step == 0)
    def _():
        acc[...] = jnp.zeros_like(acc)

    right = jnp.concatenate([g_ref[i] for i in range(step_q)], axis=1)
    for m in range(LAGS * count // tile):
        left = jnp.concatenate(
            [
                x_ref[pl.ds(pl.multiple_of((step * step_q + i) * count + m * tile, 16), tile), :]
                for i in range(step_q)
            ],
            axis=1,
        )
        part = lax.dot_general(left, right, NT_DIMS, preferred_element_type=F32)
        for h in range(total_rows // 128):
            acc[h, m * tile : (m + 1) * tile, :] += part[:, 128 * h : 128 * (h + 1)]

    @pl.when(step == pl.num_programs(0) - 1)
    def _():
        place_rows(rows_ref, acc, out_ref, count)


def correlate(x, gathered, exposure_per_row):
    total_rows = gathered.shape[1]
    count = x.shape[0] // (Q + LAGS)
    step_q = 8
    return pl.pallas_call(
        functools.partial(correlate_kernel, step_q),
        grid=(Q // step_q,),
        out_shape=jax.ShapeDtypeStruct((total_rows, count * LAGS), F32),
        in_specs=[
            pl.BlockSpec((1, total_rows), lambda s: (0, 0)),
            pl.BlockSpec(x.shape, lambda s: (0, 0)),
            pl.BlockSpec((step_q, total_rows, R), lambda s: (s, 0, 0)),
        ],
        out_specs=pl.BlockSpec((total_rows, count * LAGS), lambda s: (0, 0)),
        scratch_shapes=[pltpu.VMEM((total_rows // 128, LAGS * count, 128), F32)],
        compiler_params=pltpu.CompilerParams(vmem_limit_bytes=40 * 2**20),
        name="correlate",
    )(exposure_per_row.reshape(1, total_rows), x, gathered)


def column_sums(mine, psum):
    kind = lax.broadcasted_iota(jnp.int32, (16, 256), 0)
    lane = lax.broadcasted_iota(jnp.int32, (16, 256), 1)
    pick = (lane // 16 == kind).astype(BF16)
    for j in range(Q // 16):
        part = mine[16 * j : 16 * (j + 1)].reshape(256, R)
        good = (part.astype(F32) > 0).astype(BF16)
        for i, what in enumerate((part, good)):
            psum[j // 4, i, 16 * (j % 4) : 16 * (j % 4 + 1), :] = lax.dot_general(
                pick, what, (((1,), (0,)), ((), ())), preferred_element_type=F32
            )


def row_scales(mine, means):
    zero = jnp.zeros((16, R), F32)

    def add(j, total):
        for i in range(16):
            flux = mine[16 * j + i].astype(F32)
            resid = jnp.where(flux > 0, flux - means[j, i : i + 1, :], 0.0)
            total = total + resid * resid
        return total

    total = lax.fori_loop(0, Q // 16, add, zero)
    return lax.rsqrt(jnp.sum(total, axis=1, keepdims=True) / PIX + 1e-06)


def diagonal():
    row = lax.broadcasted_iota(jnp.int32, (16, R), 0)
    lane = lax.broadcasted_iota(jnp.int32, (16, R), 1)
    return row == lane


def store_body(smooth, x, count):
    x[0, LAGS // 2 : LAGS // 2 + Q] = smooth[...].reshape(Q, count, R).astype(BF16)


def store_margins(x, tt):
    half = LAGS // 2
    count = x.shape[2]
    lane = lax.broadcasted_iota(jnp.int32, (half * count, R), 1)

    def rolled(first, shift, edge):
        part = x[tt, first : first + half].reshape(half * count, R).astype(F32)
        part = jnp.where(lane == edge, 0.0, pltpu.roll(part, shift, 1))
        return part.astype(BF16).reshape(half, count, R)

    x[tt, :half] = rolled(Q, 1, 0)
    x[tt, half + Q :] = rolled(half, R - 1, R - 1)


def cross_kernel(
    mine,
    index_ref,
    table_ref,
    templates_ref,
    out_ref,
    raw,
    ready,
    x,
    partner,
    psum,
    tsum,
    csum,
    rsum,
    means,
    row_scale,
    scale,
    bands,
    chunks,
    smooth,
    raw_send,
    raw_recv,
    x_sem,
    r_send,
    r_recv,
    t_sem,
    s_send,
    s_recv,
    m_send,
    m_recv,
    v_send,
    v_recv,
    tail,
    tail_sem,
):
    me = lax.axis_index("blk")
    z, y, c = me // 4, (me // 2) % 2, me % 2
    planes = 4
    count = templates_ref.shape[0]
    span = Q // CHUNKS

    def blk(zz, yy, cc):
        return (zz * 2 + yy) * 2 + cc

    up, down = blk(z + 1, y, c), blk(z - 1, y, c)
    beside, twin = blk(z, 1 - y, c), blk(z, y, 1 - c)
    middle = (z == 1) | (z == 2)
    has_up, has_down = z < planes - 1, z > 0

    def remote(src, dst, send, recv, to):
        return pltpu.make_async_remote_copy(
            src_ref=src,
            dst_ref=dst,
            send_sem=send,
            recv_sem=recv,
            device_id={"blk": to},
            device_id_type=MESH,
        )

    barrier = pltpu.get_barrier_semaphore()

    def greet(o, _):
        pl.semaphore_signal(
            barrier, inc=1, device_id={"blk": lax.rem(me + o, 16)}, device_id_type=MESH
        )
        return 0

    lax.fori_loop(1, 16, greet, 0)
    raw[z, c] = mine[...]
    pl.semaphore_wait(barrier, 15)

    def raw_copy(zs, k, kind, to):
        part = raw.at[zs, c, pl.ds(k * span, span)]
        return remote(
            part, part, raw_send.at[kind, zs, k], raw_recv.at[zs * 2 + c, k], to
        )

    def from_twin(zs, k):
        part = raw.at[zs, 1 - c, pl.ds(k * span, span)]
        remote(
            part, part, raw_send.at[2, zs, k], raw_recv.at[zs * 2 + 1 - c, k], twin
        ).wait_recv()

    def on_sides(h, act):
        for sign in (1, -1):
            zs = z + sign * h
            pl.when((zs >= 0) & (zs < planes))(functools.partial(act, zs, sign))

    def send(s):
        h, k = s // CHUNKS, s % CHUNKS
        if h == 0:
            pl.when(has_up)(lambda: raw_copy(z, k, 0, up).start())
            pl.when(has_down)(lambda: raw_copy(z, k, 1, down).start())
            raw_copy(z, k, 2, twin).start()
        elif h < planes - 1:

            def onward(zs, sign):
                if sign > 0:
                    pl.when(has_down)(lambda: raw_copy(zs, k, 1, down).start())
                else:
                    pl.when(has_up)(lambda: raw_copy(zs, k, 0, up).start())

            on_sides(h, onward)

    def arrive(s):
        h, k = s // CHUNKS + 1, s % CHUNKS

        def land(zs, sign):
            raw_copy(zs, k, 2, twin).wait_recv()
            raw_copy(zs, k, 2, twin).start()

        on_sides(h, land)

    def step(s, lead):
        arrive(s)
        send(s + lead)

    send(0)
    send(1)

    column_sums(mine, psum)
    to_twin = remote(psum.at[1 - c], tsum, t_sem.at[0], t_sem.at[1], twin)
    to_twin.start()
    spread_templates(table_ref, templates_ref, bands, chunks)

    def owner(w):
        return blk(1 + w // 2, w % 2, c)

    def sum_copy(w):
        return remote(
            csum.at[w], rsum.at[z * 2 + y], s_send.at[w], s_recv.at[z * 2 + y], owner(w)
        )

    def sum_from(i):
        return remote(csum.at[0], rsum.at[i], s_send.at[0], s_recv.at[i], twin)

    def mean_copy(w, o):
        part = means.at[4 * c + w]
        chip = lax.rem(z * 2 + y + o, 8)
        return remote(
            part, part, m_send.at[o], m_recv.at[w], blk(chip // 2, chip % 2, c)
        )

    mine_w = (z - 1) * 2 + y

    def sums_to_owners():
        to_twin.wait_recv()
        for w in range(4):
            rows = slice(16 * w, 16 * (w + 1))
            csum[w] = psum[c, :, rows, :] + tsum[:, rows, :]
            away = jnp.logical_not(middle & (mine_w == w))
            pl.when(away)(lambda: sum_copy(w).start())

            @pl.when(jnp.logical_not(away))
            def _():
                rsum[z * 2 + y] = csum[w]

    def means_from_owner():
        @pl.when(middle)
        def _():
            for i in range(8):
                pl.when(z * 2 + y != i)(lambda: sum_from(i).wait_recv())
            total = rsum[0]
            for i in range(1, 8):
                total = total + rsum[i]
            means[4 * c + mine_w] = total[0] / jnp.maximum(total[1], 1.0)
            for o in range(1, 8):
                mean_copy(mine_w, o).start()

    half_means = remote(
        means.at[pl.ds(4 * c, 4)],
        means.at[pl.ds(4 * c, 4)],
        t_sem.at[2],
        t_sem.at[3],
        twin,
    )

    def means_to_twin():
        for w in range(4):
            away = jnp.logical_not(middle & (mine_w == w))
            pl.when(away)(lambda: mean_copy(w, 1).wait_recv())
        half_means.start()

    def scale_copy(o):
        at = lax.rem(z * 2 + c + o, 8)
        return remote(
            row_scale.at[z * 2 + c],
            row_scale.at[z * 2 + c],
            v_send.at[o],
            v_recv.at[z * 2 + c],
            blk(at // 2, y, at % 2),
        )

    def scales_out():
        half_means.wait_recv()
        own = row_scales(mine, means)
        row_scale[z * 2 + c] = jnp.sum(
            jnp.where(diagonal(), own, 0.0), axis=0, keepdims=True
        )
        for o in range(1, 8):
            scale_copy(o).start()

    def scales_in():
        for i in range(8):
            part = row_scale.at[i]
            pl.when(z * 2 + c != i)(
                lambda: remote(part, part, v_send.at[0], v_recv.at[i], twin).wait_recv()
            )
            column = jnp.sum(
                jnp.where(diagonal(), row_scale[i], 0.0), axis=1, keepdims=True
            )
            scale[i] = jnp.broadcast_to(column, (16, R))

    def x_copy(k):
        rows = pl.ds(LAGS // 2 + k * span, span)
        return remote(
            x.at[0, rows], x.at[1, rows], x_sem.at[0, k], x_sem.at[1, k], beside
        )

    smooth_templates(index_ref, bands, chunks, smooth, 0, 2, count)
    sums_to_owners()
    send(2)
    send(3)
    smooth_templates(index_ref, bands, chunks, smooth, 2, count, count)
    store_body(smooth, x, count)
    x_copy(0).start()
    for zs in range(planes):
        ready[zs, :AHEAD] = jnp.zeros((AHEAD, 32, R), BF16)
        ready[zs, AHEAD + Q :] = jnp.zeros((ready.shape[1] - AHEAD - Q, 32, R), BF16)
    store_margins(x, 0)
    after = {2: means_from_owner, 5: means_to_twin, 6: scales_out, 9: scales_in}
    for s in range(10):
        step(s, LEAD)
        if 0 < s + 1 < CHUNKS:
            x_copy(s + 1).start()
        after.get(s, lambda: None)()
    for s in range(10 + LEAD, 18):
        send(s)

    def normalise(zs, first, last):
        for cc in range(2):
            factor = scale[zs * 2 + cc]

            def tile(j, _):
                for i in range(16):
                    flux = raw[zs, cc, 16 * j + i].astype(F32)
                    resid = jnp.where(flux > 0, flux - means[j, i : i + 1, :], 0.0)
                    ready[zs, AHEAD + 16 * j + i, 16 * cc : 16 * (cc + 1), :] = (
                        resid * factor
                    ).astype(BF16)
                return 0

            lax.fori_loop(first, last, tile, 0)

    def product(zs, first, last, ends=False):
        right = jnp.concatenate(
            [ready[zs, i : i + 8].reshape(256, R) for i in range(first, last)], axis=1
        )
        left = jnp.concatenate(
            [
                jnp.concatenate(
                    [x[tt, i + 8 * a] for tt in range(2) for a in range(8)], axis=0
                )
                for i in range(first, last)
            ],
            axis=1,
        )
        part = lax.dot_general(left, right, NT_DIMS, preferred_element_type=F32)
        if ends:
            out_ref[zs * 2 + y] += part[:128]
            tail[0] = part[128:].astype(BF16)
        elif first == 0:
            out_ref[zs * 2 + y] = part[:128]
            partner[zs] = part[128:]
        else:
            out_ref[zs * 2 + y] += part[:128]
            partner[zs] += part[128:]

    def result_copy(zs):
        return remote(
            partner.at[zs], out_ref.at[zs * 2 + y], r_send.at[zs], r_recv.at[zs], beside
        )

    def slot(i):
        near = jnp.where(z < 2, z + 1, z - 1)
        far = jnp.where(z == 0, 2, jnp.where(z == 1, 0, jnp.where(z == 2, 3, 1)))
        end = jnp.where(z < 2, 3, 0)
        return jnp.where(
            i == 0, z, jnp.where(i == 1, near, jnp.where(i == 2, far, end))
        )

    def block(i, _):
        zs = slot(i)

        @pl.when(i == 0)
        def _():
            for k in range(CHUNKS):
                x_copy(k).wait_recv()
            store_margins(x, 1)

        @pl.when(i == 1)
        def _():
            for s in range(10, 14):
                step(s, 8)

        @pl.when(i == 2)
        def _():
            for s in range(14, 16):
                step(s, 8)

        for k in range(CHUNKS):
            from_twin(zs, k)
        normalise(zs, 0, Q // 16)

        @pl.when(z < planes)
        def _():
            for quarter in range(4):
                product(zs, 32 * quarter, 32 * quarter + (32 if quarter < 3 else 40))

        result_copy(zs).start()
        return 0

    lax.fori_loop(0, 3, block, 0)
    last = slot(3)
    for first, end in PIECES:
        for k in range(first, end):
            arrive(16 + k)
        for k in range(first, end):
            from_twin(last, k)
        normalise(last, first, end)
        ends = end == CHUNKS
        low, high = span * first, span * end + (8 if ends else 0)
        pl.when(z < planes)(functools.partial(product, last, low, high, ends))
        if first == PIECES[-2][0]:
            result_copy(last).start()
    tail_copy = remote(tail.at[0], tail.at[1], tail_sem.at[0], tail_sem.at[1], beside)
    tail_copy.start()

    for k in range(CHUNKS):
        x_copy(k).wait_send()
    to_twin.wait_send()
    half_means.wait_send()
    for w in range(4):
        away = jnp.logical_not(middle & (mine_w == w))
        pl.when(away)(lambda: sum_copy(w).wait_send())

    @pl.when(middle)
    def _():
        for o in range(1, 8):
            mean_copy(mine_w, o).wait_send()

    for o in range(1, 8):
        scale_copy(o).wait_send()

    def sent(k, _):
        for zs in range(planes):
            raw_copy(zs, k, 2, twin).wait_send()
            pl.when(has_up & (zs <= z))(lambda: raw_copy(zs, k, 0, up).wait_send())
            pl.when(has_down & (zs >= z))(lambda: raw_copy(zs, k, 1, down).wait_send())
        return 0

    lax.fori_loop(0, CHUNKS, sent, 0)
    for zs in range(planes):
        result_copy(zs).wait_send()
    tail_copy.wait_send()
    for zs in range(planes):
        result_copy(zs).wait_recv()
    tail_copy.wait_recv()
    out_ref[last * 2 + 1 - y] += tail[1].astype(F32)


def cross(masked, templates, template_kernel_index, line_spread_table):
    count = templates.shape[0]
    rows = masked.shape[1]
    vmem = pl.BlockSpec(memory_space=pltpu.VMEM)
    dma = pltpu.SemaphoreType.DMA
    return pl.pallas_call(
        cross_kernel,
        out_shape=jax.ShapeDtypeStruct((8, 8 * count, 256), F32),
        in_specs=[vmem, pl.BlockSpec(memory_space=pltpu.SMEM), vmem, vmem],
        out_specs=vmem,
        scratch_shapes=[
            pltpu.VMEM((4, 2, Q, rows, R), BF16),
            pltpu.VMEM((4, Q + 16, 2 * rows, R), BF16),
            pltpu.VMEM((2, Q + LAGS, count, R), BF16),
            pltpu.VMEM((4, 8 * count, 256), F32),
            pltpu.VMEM((2, 2, Q // 2, R), F32),
            pltpu.VMEM((2, Q // 2, R), F32),
            pltpu.VMEM((4, 2, 16, R), F32),
            pltpu.VMEM((8, 2, 16, R), F32),
            pltpu.VMEM((8, 16, R), F32),
            pltpu.VMEM((8, 1, R), F32),
            pltpu.VMEM((8, 16, R), F32),
            pltpu.VMEM((KERNELS, Q, 2 * BAND), BF16),
            pltpu.VMEM((BAND // 128, R * count, 128), F32),
            pltpu.VMEM((Q * count, R), F32),
            dma((3, 4, CHUNKS)),
            dma((8, CHUNKS)),
            dma((2, CHUNKS)),
            dma((4,)),
            dma((4,)),
            dma((4,)),
            dma((4,)),
            dma((8,)),
            dma((8,)),
            dma((4,)),
            dma((8,)),
            dma((8,)),
            pltpu.VMEM((2, 8 * count, 256), BF16),
            dma((2,)),
        ],
        compiler_params=pltpu.CompilerParams(
            collective_id=0, has_side_effects=True, vmem_limit_bytes=48 * 2**20
        ),
        name="cross",
    )(masked, template_kernel_index, line_spread_table, templates)


def place_kernel(rows_ref, part_ref, out_ref, split):
    count = part_ref.shape[1] // 8
    lane = lax.broadcasted_iota(jnp.int32, (8 * count, 128), 1) // 32
    for h in range(2):
        for b in range(8):
            at = 7 - b
            piece = None
            for i in range(4):
                one = part_ref[4 * h + i, :, 128 * (at // 4) : 128 * (at // 4 + 1)]
                shift = 32 * (i - at % 4) % 128
                one = pltpu.roll(one, shift, 1) if shift else one
                piece = one if piece is None else jnp.where(lane == i, one, piece)
            for a in range(8):
                split[h, (8 * a + b) * count : (8 * a + b + 1) * count, :] = piece[
                    a * count : (a + 1) * count
                ]
    place_rows(rows_ref, split, out_ref, count)


def place(parts, exposure_per_row):
    total_rows = 32 * parts.shape[0]
    across = parts.shape[1] * 8
    return pl.pallas_call(
        place_kernel,
        out_shape=jax.ShapeDtypeStruct((total_rows, across), F32),
        in_specs=[pl.BlockSpec(memory_space=pltpu.VMEM)] * 2,
        out_specs=pl.BlockSpec(memory_space=pltpu.VMEM),
        scratch_shapes=[pltpu.VMEM((total_rows // 128, across, 128), F32)],
        compiler_params=pltpu.CompilerParams(vmem_limit_bytes=16 * 2**20),
        name="place",
    )(exposure_per_row.reshape(1, total_rows), parts)


def shards(
    devices,
    observed,
    good_pixel_mask,
    templates,
    template_kernel_index,
    line_spread_table,
    exposure_per_row,
):
    rows = observed.shape[0]
    flux = jnp.where(good_pixel_mask > 0, observed, 0)
    if devices == 16 and rows == 16 and templates.shape[0] == 16:
        masked = flux.reshape(rows, R, Q).transpose(2, 0, 1)
        parts = cross(masked, templates, template_kernel_index, line_spread_table)
        return place(parts, exposure_per_row)
    flux = flux.astype(F32)
    present = (flux > 0).astype(F32)
    sums, counts = jnp.sum(flux, axis=0), jnp.sum(present, axis=0)
    x = shape_templates(templates, template_kernel_index, line_spread_table)
    sums = lax.psum(jnp.stack([sums, counts]), "blk")
    mean = sums[0] / jnp.maximum(sums[1], 1.0)
    resid = present * (flux - mean[None, :])
    scale = lax.rsqrt(jnp.sum(resid * resid, axis=1) / PIX + 1e-06)
    ready = (resid * scale[:, None]).astype(BF16)
    ready = ready.reshape(rows, R, Q).transpose(2, 0, 1)
    gathered = lax.all_gather(ready, "blk", axis=1, tiled=True)
    return correlate(x, gathered, exposure_per_row)


def solution(mesh):
    in_specs = (
        P(("grp", "blk"), None),
        P(("grp", "blk"), None),
        P(("grp", "blk"), None),
        P(("grp", "blk")),
        P(),
        P("grp"),
    )
    out_specs = P("grp", "blk")
    return jax.shard_map(
        functools.partial(shards, mesh.shape["blk"]),
        mesh=mesh,
        in_specs=in_specs,
        out_specs=out_specs,
        check_vma=False,
    )
```

```python
import functools
import math

import jax
import jax.numpy as jnp
from jax import lax
from jax.experimental import pallas as pl
from jax.experimental.pallas import tpu as pltpu
from jax.sharding import PartitionSpec as P

PIX = 16384
LAGS = 64
TAPS = 97
KERNELS = 8
Q = 128
R = PIX // Q
BAND = 640
CHUNKS = 8
LEAD = 4
AHEAD = 7
PIECES = ((0, 4), (4, 6), (6, 8))
F32 = jnp.float32
BF16 = jnp.bfloat16
MESH = pl.DeviceIdType.MESH
NT_DIMS = (((1,), (1,)), ((), ()))


def template_kernel(index_ref, table_ref, templates_ref, x_ref, bands, chunks, smooth):
    count = templates_ref.shape[0]
    spread_templates(table_ref, templates_ref, bands, chunks)
    smooth_templates(index_ref, bands, chunks, smooth, 0, count, count)
    pack_templates(smooth, x_ref, count)


def spread_templates(table_ref, templates_ref, bands, chunks):
    count = templates_ref.shape[0]
    for k in range(KERNELS):
        row = jnp.concatenate(
            [table_ref[k : k + 1, :], jnp.zeros((1, BAND - TAPS), F32)], axis=1
        )
        row = jnp.broadcast_to(row, (Q, BAND))
        band = pltpu.roll(row, 0, 1, stride=4, stride_axis=0)
        high = band.astype(BF16)
        bands[k, :, :BAND] = high
        bands[k, :, BAND:] = (band - high.astype(F32)).astype(BF16)

    def spread(r, _):
        at = pl.multiple_of(r * (4 * Q), 128)
        piece = templates_ref[:, pl.ds(at, BAND)].astype(F32)
        for i in range(BAND // 128):
            chunks[i, pl.ds(pl.multiple_of(r * count, count), count), :] = piece[
                :, 128 * i : 128 * (i + 1)
            ]
        return 0

    lax.fori_loop(0, R - 1, spread, 0, unroll=8)
    last = (R - 1) * 4 * Q
    left = templates_ref.shape[1] - last
    tail = templates_ref[:, last:].astype(F32)
    tail = jnp.concatenate([tail, jnp.zeros((count, BAND - left), F32)], axis=1)
    for i in range(BAND // 128):
        chunks[i, (R - 1) * count :, :] = tail[:, 128 * i : 128 * (i + 1)]


def smooth_templates(index_ref, bands, chunks, smooth, first, last, count):
    for t in range(first, last):
        rows = [
            chunks[i, pl.ds(t, R, stride=count), :].astype(BF16) for i in range(BAND // 128)
        ]
        rows = jnp.concatenate(rows + rows, axis=1)
        flux = lax.dot_general(
            bands[index_ref[t]], rows, NT_DIMS, preferred_element_type=F32
        )
        total = jnp.sum(flux * flux)
        smooth[pl.ds(t, Q, stride=count), :] = flux * lax.rsqrt(
            jnp.full((1, 1), total) / PIX + 1e-06
        )


def pack_templates(smooth, x_ref, count):
    half = LAGS // 2
    body = smooth[...]
    lane = lax.broadcasted_iota(jnp.int32, (half * count, R), 1)
    x_ref[half * count : (half + Q) * count, :] = body.astype(BF16)
    before = pltpu.roll(body[(Q - half) * count :, :], 1, 1)
    x_ref[: half * count, :] = jnp.where(lane == 0, 0.0, before).astype(BF16)
    after = pltpu.roll(body[: half * count, :], R - 1, 1)
    x_ref[(half + Q) * count :, :] = jnp.where(lane == R - 1, 0.0, after).astype(BF16)


def shape_templates(templates, template_kernel_index, line_spread_table):
    count = templates.shape[0]
    return pl.pallas_call(
        template_kernel,
        out_shape=jax.ShapeDtypeStruct(((Q + LAGS) * count, R), BF16),
        in_specs=[
            pl.BlockSpec(memory_space=pltpu.SMEM),
            pl.BlockSpec(memory_space=pltpu.VMEM),
            pl.BlockSpec(memory_space=pltpu.VMEM),
        ],
        out_specs=pl.BlockSpec(memory_space=pltpu.VMEM),
        scratch_shapes=[
            pltpu.VMEM((KERNELS, Q, 2 * BAND), BF16),
            pltpu.VMEM((BAND // 128, R * count, 128), F32),
            pltpu.VMEM((Q * count, R), F32),
        ],
        compiler_params=pltpu.CompilerParams(vmem_limit_bytes=40 * 2**20),
        cost_estimate=pl.CostEstimate(
            flops=2 * count * Q * R * 2 * BAND, bytes_accessed=6 * 2**20, transcendentals=0
        ),
        name="shape_templates",
    )(template_kernel_index, line_spread_table, templates)


def place_rows(rows_ref, acc, out_ref, count, group=0, groups=1):
    total_rows = rows_ref.shape[1]
    chosen = (
        lax.broadcasted_iota(jnp.int32, (total_rows, total_rows), 0) == rows_ref[...]
    ).astype(BF16)
    both = jnp.concatenate([chosen, chosen], axis=1)
    for t in range(group * count // groups, (group + 1) * count // groups, 2):
        part = jnp.concatenate(
            [
                jnp.concatenate(
                    [
                        acc[h, pl.ds(t + i, LAGS, stride=count), :]
                        for h in range(total_rows // 128)
                    ],
                    axis=1,
                )
                for i in range(2)
            ],
            axis=0,
        ) * F32(1.0 / math.sqrt(PIX))
        high = part.astype(BF16)
        low = (part - high.astype(F32)).astype(BF16)
        out_ref[:, t * LAGS : (t + 2) * LAGS] = lax.dot_general(
            both,
            jnp.concatenate([high, low], axis=1),
            NT_DIMS,
            preferred_element_type=F32,
        )


def correlate_kernel(step_q, rows_ref, x_ref, g_ref, out_ref, acc):
    step = pl.program_id(0)
    total_rows = rows_ref.shape[1]
    count = x_ref.shape[0] // (Q + LAGS)
    tile = 256

    @pl.when(step == 0)
    def _():
        acc[...] = jnp.zeros_like(acc)

    right = jnp.concatenate([g_ref[i] for i in range(step_q)], axis=1)
    for m in range(LAGS * count // tile):
        left = jnp.concatenate(
            [
                x_ref[pl.ds(pl.multiple_of((step * step_q + i) * count + m * tile, 16), tile), :]
                for i in range(step_q)
            ],
            axis=1,
        )
        part = lax.dot_general(left, right, NT_DIMS, preferred_element_type=F32)
        for h in range(total_rows // 128):
            acc[h, m * tile : (m + 1) * tile, :] += part[:, 128 * h : 128 * (h + 1)]

    @pl.when(step == pl.num_programs(0) - 1)
    def _():
        place_rows(rows_ref, acc, out_ref, count)


def correlate(x, gathered, exposure_per_row):
    total_rows = gathered.shape[1]
    count = x.shape[0] // (Q + LAGS)
    step_q = 8
    return pl.pallas_call(
        functools.partial(correlate_kernel, step_q),
        grid=(Q // step_q,),
        out_shape=jax.ShapeDtypeStruct((total_rows, count * LAGS), F32),
        in_specs=[
            pl.BlockSpec((1, total_rows), lambda s: (0, 0)),
            pl.BlockSpec(x.shape, lambda s: (0, 0)),
            pl.BlockSpec((step_q, total_rows, R), lambda s: (s, 0, 0)),
        ],
        out_specs=pl.BlockSpec((total_rows, count * LAGS), lambda s: (0, 0)),
        scratch_shapes=[pltpu.VMEM((total_rows // 128, LAGS * count, 128), F32)],
        compiler_params=pltpu.CompilerParams(vmem_limit_bytes=40 * 2**20),
        name="correlate",
    )(exposure_per_row.reshape(1, total_rows), x, gathered)


def column_sums(mine, psum):
    kind = lax.broadcasted_iota(jnp.int32, (16, 256), 0)
    lane = lax.broadcasted_iota(jnp.int32, (16, 256), 1)
    pick = (lane // 16 == kind).astype(BF16)
    for j in range(Q // 16):
        part = mine[16 * j : 16 * (j + 1)].reshape(256, R)
        good = (part.astype(F32) > 0).astype(BF16)
        for i, what in enumerate((part, good)):
            psum[j // 4, i, 16 * (j % 4) : 16 * (j % 4 + 1), :] = lax.dot_general(
                pick, what, (((1,), (0,)), ((), ())), preferred_element_type=F32
            )


def row_scales(mine, means):
    zero = jnp.zeros((16, R), F32)

    def add(j, total):
        for i in range(16):
            flux = mine[16 * j + i].astype(F32)
            resid = jnp.where(flux > 0, flux - means[j, i : i + 1, :], 0.0)
            total = total + resid * resid
        return total

    total = lax.fori_loop(0, Q // 16, add, zero)
    return lax.rsqrt(jnp.sum(total, axis=1, keepdims=True) / PIX + 1e-06)


def diagonal():
    row = lax.broadcasted_iota(jnp.int32, (16, R), 0)
    lane = lax.broadcasted_iota(jnp.int32, (16, R), 1)
    return row == lane


def store_body(smooth, x, count):
    x[0, LAGS // 2 : LAGS // 2 + Q] = smooth[...].reshape(Q, count, R).astype(BF16)


def store_margins(x, tt):
    half = LAGS // 2
    count = x.shape[2]
    lane = lax.broadcasted_iota(jnp.int32, (half * count, R), 1)

    def rolled(first, shift, edge):
        part = x[tt, first : first + half].reshape(half * count, R).astype(F32)
        part = jnp.where(lane == edge, 0.0, pltpu.roll(part, shift, 1))
        return part.astype(BF16).reshape(half, count, R)

    x[tt, :half] = rolled(Q, 1, 0)
    x[tt, half + Q :] = rolled(half, R - 1, R - 1)


def cross_kernel(
    mine,
    index_ref,
    table_ref,
    templates_ref,
    out_ref,
    raw,
    ready,
    x,
    partner,
    psum,
    tsum,
    csum,
    rsum,
    means,
    row_scale,
    scale,
    bands,
    chunks,
    smooth,
    raw_send,
    raw_recv,
    x_sem,
    r_send,
    r_recv,
    t_sem,
    s_send,
    s_recv,
    m_send,
    m_recv,
    v_send,
    v_recv,
    tail,
    tail_sem,
):
    me = lax.axis_index("blk")
    z, y, c = me // 4, (me // 2) % 2, me % 2
    planes = 4
    count = templates_ref.shape[0]
    span = Q // CHUNKS

    def blk(zz, yy, cc):
        return (zz * 2 + yy) * 2 + cc

    up, down = blk(z + 1, y, c), blk(z - 1, y, c)
    beside, twin = blk(z, 1 - y, c), blk(z, y, 1 - c)
    middle = (z == 1) | (z == 2)
    has_up, has_down = z < planes - 1, z > 0

    def remote(src, dst, send, recv, to):
        return pltpu.make_async_remote_copy(
            src_ref=src,
            dst_ref=dst,
            send_sem=send,
            recv_sem=recv,
            device_id={"blk": to},
            device_id_type=MESH,
        )

    barrier = pltpu.get_barrier_semaphore()

    def greet(o, _):
        pl.semaphore_signal(
            barrier, inc=1, device_id={"blk": lax.rem(me + o, 16)}, device_id_type=MESH
        )
        return 0

    lax.fori_loop(1, 16, greet, 0)
    raw[z, c] = mine[...]
    pl.semaphore_wait(barrier, 15)

    def raw_copy(zs, k, kind, to):
        part = raw.at[zs, c, pl.ds(k * span, span)]
        return remote(
            part, part, raw_send.at[kind, zs, k], raw_recv.at[zs * 2 + c, k], to
        )

    def from_twin(zs, k):
        part = raw.at[zs, 1 - c, pl.ds(k * span, span)]
        remote(
            part, part, raw_send.at[2, zs, k], raw_recv.at[zs * 2 + 1 - c, k], twin
        ).wait_recv()

    def on_sides(h, act):
        for sign in (1, -1):
            zs = z + sign * h
            pl.when((zs >= 0) & (zs < planes))(functools.partial(act, zs, sign))

    def send(s):
        h, k = s // CHUNKS, s % CHUNKS
        if h == 0:
            pl.when(has_up)(lambda: raw_copy(z, k, 0, up).start())
            pl.when(has_down)(lambda: raw_copy(z, k, 1, down).start())
            raw_copy(z, k, 2, twin).start()
        elif h < planes - 1:

            def onward(zs, sign):
                if sign > 0:
                    pl.when(has_down)(lambda: raw_copy(zs, k, 1, down).start())
                else:
                    pl.when(has_up)(lambda: raw_copy(zs, k, 0, up).start())

            on_sides(h, onward)

    def arrive(s):
        h, k = s // CHUNKS + 1, s % CHUNKS

        def land(zs, sign):
            raw_copy(zs, k, 2, twin).wait_recv()
            raw_copy(zs, k, 2, twin).start()

        on_sides(h, land)

    def step(s, lead):
        arrive(s)
        send(s + lead)

    send(0)
    send(1)

    column_sums(mine, psum)
    to_twin = remote(psum.at[1 - c], tsum, t_sem.at[0], t_sem.at[1], twin)
    to_twin.start()
    spread_templates(table_ref, templates_ref, bands, chunks)

    def owner(w):
        return blk(1 + w // 2, w % 2, c)

    def sum_copy(w):
        return remote(
            csum.at[w], rsum.at[z * 2 + y], s_send.at[w], s_recv.at[z * 2 + y], owner(w)
        )

    def sum_from(i):
        return remote(csum.at[0], rsum.at[i], s_send.at[0], s_recv.at[i], twin)

    def mean_copy(w, o):
        part = means.at[4 * c + w]
        chip = lax.rem(z * 2 + y + o, 8)
        return remote(
            part, part, m_send.at[o], m_recv.at[w], blk(chip // 2, chip % 2, c)
        )

    mine_w = (z - 1) * 2 + y

    def sums_to_owners():
        to_twin.wait_recv()
        for w in range(4):
            rows = slice(16 * w, 16 * (w + 1))
            csum[w] = psum[c, :, rows, :] + tsum[:, rows, :]
            away = jnp.logical_not(middle & (mine_w == w))
            pl.when(away)(lambda: sum_copy(w).start())

            @pl.when(jnp.logical_not(away))
            def _():
                rsum[z * 2 + y] = csum[w]

    def means_from_owner():
        @pl.when(middle)
        def _():
            for i in range(8):
                pl.when(z * 2 + y != i)(lambda: sum_from(i).wait_recv())
            total = rsum[0]
            for i in range(1, 8):
                total = total + rsum[i]
            means[4 * c + mine_w] = total[0] / jnp.maximum(total[1], 1.0)
            for o in range(1, 8):
                mean_copy(mine_w, o).start()

    half_means = remote(
        means.at[pl.ds(4 * c, 4)],
        means.at[pl.ds(4 * c, 4)],
        t_sem.at[2],
        t_sem.at[3],
        twin,
    )

    def means_to_twin():
        for w in range(4):
            away = jnp.logical_not(middle & (mine_w == w))
            pl.when(away)(lambda: mean_copy(w, 1).wait_recv())
        half_means.start()

    def scale_copy(o):
        at = lax.rem(z * 2 + c + o, 8)
        return remote(
            row_scale.at[z * 2 + c],
            row_scale.at[z * 2 + c],
            v_send.at[o],
            v_recv.at[z * 2 + c],
            blk(at // 2, y, at % 2),
        )

    def scales_out():
        half_means.wait_recv()
        own = row_scales(mine, means)
        row_scale[z * 2 + c] = jnp.sum(
            jnp.where(diagonal(), own, 0.0), axis=0, keepdims=True
        )
        for o in range(1, 8):
            scale_copy(o).start()

    def scales_in():
        for i in range(8):
            part = row_scale.at[i]
            pl.when(z * 2 + c != i)(
                lambda: remote(part, part, v_send.at[0], v_recv.at[i], twin).wait_recv()
            )
            column = jnp.sum(
                jnp.where(diagonal(), row_scale[i], 0.0), axis=1, keepdims=True
            )
            scale[i] = jnp.broadcast_to(column, (16, R))

    def x_copy(k):
        rows = pl.ds(LAGS // 2 + k * span, span)
        return remote(
            x.at[0, rows], x.at[1, rows], x_sem.at[0, k], x_sem.at[1, k], beside
        )

    smooth_templates(index_ref, bands, chunks, smooth, 0, 2, count)
    sums_to_owners()
    send(2)
    send(3)
    smooth_templates(index_ref, bands, chunks, smooth, 2, count, count)
    store_body(smooth, x, count)
    x_copy(0).start()
    for zs in range(planes):
        ready[zs, :AHEAD] = jnp.zeros((AHEAD, 32, R), BF16)
        ready[zs, AHEAD + Q :] = jnp.zeros((ready.shape[1] - AHEAD - Q, 32, R), BF16)
    store_margins(x, 0)
    after = {2: means_from_owner, 5: means_to_twin, 6: scales_out, 9: scales_in}
    for s in range(10):
        step(s, LEAD if s < 8 else 8)
        if 0 < s + 1 < CHUNKS:
            x_copy(s + 1).start()
        after.get(s, lambda: None)()
        if s == 7:
            for e in range(8 + LEAD, 8 + 8):
                send(e)

    def normalise(zs, first, last):
        for cc in range(2):
            factor = scale[zs * 2 + cc]

            def tile(j, _):
                for i in range(16):
                    flux = raw[zs, cc, 16 * j + i].astype(F32)
                    resid = jnp.where(flux > 0, flux - means[j, i : i + 1, :], 0.0)
                    ready[zs, AHEAD + 16 * j + i, 16 * cc : 16 * (cc + 1), :] = (
                        resid * factor
                    ).astype(BF16)
                return 0

            lax.fori_loop(first, last, tile, 0)

    def product(zs, first, last, ends=False):
        right = jnp.concatenate(
            [ready[zs, i : i + 8].reshape(256, R) for i in range(first, last)], axis=1
        )
        left = jnp.concatenate(
            [
                jnp.concatenate(
                    [x[tt, i + 8 * a] for tt in range(2) for a in range(8)], axis=0
                )
                for i in range(first, last)
            ],
            axis=1,
        )
        part = lax.dot_general(left, right, NT_DIMS, preferred_element_type=F32)
        if ends:
            out_ref[zs * 2 + y] += part[:128]
            tail[0] = part[128:].astype(BF16)
        elif first == 0:
            out_ref[zs * 2 + y] = part[:128]
            partner[zs] = part[128:]
        else:
            out_ref[zs * 2 + y] += part[:128]
            partner[zs] += part[128:]

    def result_copy(zs):
        return remote(
            partner.at[zs], out_ref.at[zs * 2 + y], r_send.at[zs], r_recv.at[zs], beside
        )

    def slot(i):
        near = jnp.where(z < 2, z + 1, z - 1)
        far = jnp.where(z == 0, 2, jnp.where(z == 1, 0, jnp.where(z == 2, 3, 1)))
        end = jnp.where(z < 2, 3, 0)
        return jnp.where(
            i == 0, z, jnp.where(i == 1, near, jnp.where(i == 2, far, end))
        )

    def block(i, _):
        zs = slot(i)

        @pl.when(i == 1)
        def _():
            for s in range(10, 14):
                step(s, 8)

        @pl.when(i == 2)
        def _():
            for s in range(14, 16):
                step(s, 8)

        for k in range(CHUNKS):
            from_twin(zs, k)
        normalise(zs, 0, Q // 16)

        @pl.when(i == 0)
        def _():
            for k in range(CHUNKS):
                x_copy(k).wait_recv()
            store_margins(x, 1)

        @pl.when(z < planes)
        def _():
            for quarter in range(4):
                product(zs, 32 * quarter, 32 * quarter + (32 if quarter < 3 else 40))

        result_copy(zs).start()
        return 0

    lax.fori_loop(0, 3, block, 0)
    last = slot(3)
    for first, end in PIECES:
        for k in range(first, end):
            arrive(16 + k)
        for k in range(first, end):
            from_twin(last, k)
        normalise(last, first, end)
        ends = end == CHUNKS
        low, high = span * first, span * end + (8 if ends else 0)
        pl.when(z < planes)(functools.partial(product, last, low, high, ends))
        if first == PIECES[-2][0]:
            result_copy(last).start()
    tail_copy = remote(tail.at[0], tail.at[1], tail_sem.at[0], tail_sem.at[1], beside)
    tail_copy.start()

    for k in range(CHUNKS):
        x_copy(k).wait_send()
    to_twin.wait_send()
    half_means.wait_send()
    for w in range(4):
        away = jnp.logical_not(middle & (mine_w == w))
        pl.when(away)(lambda: sum_copy(w).wait_send())

    @pl.when(middle)
    def _():
        for o in range(1, 8):
            mean_copy(mine_w, o).wait_send()

    for o in range(1, 8):
        scale_copy(o).wait_send()

    def sent(k, _):
        for zs in range(planes):
            raw_copy(zs, k, 2, twin).wait_send()
            pl.when(has_up & (zs <= z))(lambda: raw_copy(zs, k, 0, up).wait_send())
            pl.when(has_down & (zs >= z))(lambda: raw_copy(zs, k, 1, down).wait_send())
        return 0

    lax.fori_loop(0, CHUNKS, sent, 0)
    for zs in range(planes):
        result_copy(zs).wait_send()
    tail_copy.wait_send()
    for zs in range(planes):
        result_copy(zs).wait_recv()
    tail_copy.wait_recv()
    out_ref[last * 2 + 1 - y] += tail[1].astype(F32)


def cross(masked, templates, template_kernel_index, line_spread_table):
    count = templates.shape[0]
    rows = masked.shape[1]
    vmem = pl.BlockSpec(memory_space=pltpu.VMEM)
    dma = pltpu.SemaphoreType.DMA
    return pl.pallas_call(
        cross_kernel,
        out_shape=jax.ShapeDtypeStruct((8, 8 * count, 256), F32),
        in_specs=[vmem, pl.BlockSpec(memory_space=pltpu.SMEM), vmem, vmem],
        out_specs=vmem,
        scratch_shapes=[
            pltpu.VMEM((4, 2, Q, rows, R), BF16),
            pltpu.VMEM((4, Q + 16, 2 * rows, R), BF16),
            pltpu.VMEM((2, Q + LAGS, count, R), BF16),
            pltpu.VMEM((4, 8 * count, 256), F32),
            pltpu.VMEM((2, 2, Q // 2, R), F32),
            pltpu.VMEM((2, Q // 2, R), F32),
            pltpu.VMEM((4, 2, 16, R), F32),
            pltpu.VMEM((8, 2, 16, R), F32),
            pltpu.VMEM((8, 16, R), F32),
            pltpu.VMEM((8, 1, R), F32),
            pltpu.VMEM((8, 16, R), F32),
            pltpu.VMEM((KERNELS, Q, 2 * BAND), BF16),
            pltpu.VMEM((BAND // 128, R * count, 128), F32),
            pltpu.VMEM((Q * count, R), F32),
            dma((3, 4, CHUNKS)),
            dma((8, CHUNKS)),
            dma((2, CHUNKS)),
            dma((4,)),
            dma((4,)),
            dma((4,)),
            dma((4,)),
            dma((8,)),
            dma((8,)),
            dma((4,)),
            dma((8,)),
            dma((8,)),
            pltpu.VMEM((2, 8 * count, 256), BF16),
            dma((2,)),
        ],
        compiler_params=pltpu.CompilerParams(
            collective_id=0, has_side_effects=True, vmem_limit_bytes=48 * 2**20
        ),
        name="cross",
    )(masked, template_kernel_index, line_spread_table, templates)


def place_kernel(rows_ref, part_ref, out_hbm, split, out_ref, sem):
    count = part_ref.shape[1] // 8
    lane = lax.broadcasted_iota(jnp.int32, (8 * count, 128), 1) // 32
    for h in range(2):
        for b in range(8):
            at = 7 - b
            piece = None
            for i in range(4):
                one = part_ref[4 * h + i, :, 128 * (at // 4) : 128 * (at // 4 + 1)]
                shift = 32 * (i - at % 4) % 128
                one = pltpu.roll(one, shift, 1) if shift else one
                piece = one if piece is None else jnp.where(lane == i, one, piece)
            for a in range(8):
                split[h, (8 * a + b) * count : (8 * a + b + 1) * count, :] = piece[
                    a * count : (a + 1) * count
                ]
    groups = sem.shape[0]
    wide = out_ref.shape[1] // groups
    copies = []
    for g in range(groups):
        place_rows(rows_ref, split, out_ref, count, g, groups)
        at = pl.ds(g * wide, wide)
        copies.append(
            pltpu.make_async_copy(out_ref.at[:, at], out_hbm.at[:, at], sem.at[g])
        )
        copies[-1].start()
    for copy in copies:
        copy.wait()


def place(parts, exposure_per_row):
    total_rows = 32 * parts.shape[0]
    across = parts.shape[1] * 8
    return pl.pallas_call(
        place_kernel,
        out_shape=jax.ShapeDtypeStruct((total_rows, across), F32),
        in_specs=[pl.BlockSpec(memory_space=pltpu.VMEM)] * 2,
        out_specs=pl.BlockSpec(memory_space=pl.ANY),
        scratch_shapes=[
            pltpu.VMEM((total_rows // 128, across, 128), F32),
            pltpu.VMEM((total_rows, across), F32),
            pltpu.SemaphoreType.DMA((4,)),
        ],
        compiler_params=pltpu.CompilerParams(vmem_limit_bytes=16 * 2**20),
        name="place",
    )(exposure_per_row.reshape(1, total_rows), parts)


def shards(
    devices,
    observed,
    good_pixel_mask,
    templates,
    template_kernel_index,
    line_spread_table,
    exposure_per_row,
):
    rows = observed.shape[0]
    flux = jnp.where(good_pixel_mask > 0, observed, 0)
    if devices == 16 and rows == 16 and templates.shape[0] == 16:
        masked = flux.reshape(rows, R, Q).transpose(2, 0, 1)
        parts = cross(masked, templates, template_kernel_index, line_spread_table)
        return place(parts, exposure_per_row)
    flux = flux.astype(F32)
    present = (flux > 0).astype(F32)
    sums, counts = jnp.sum(flux, axis=0), jnp.sum(present, axis=0)
    x = shape_templates(templates, template_kernel_index, line_spread_table)
    sums = lax.psum(jnp.stack([sums, counts]), "blk")
    mean = sums[0] / jnp.maximum(sums[1], 1.0)
    resid = present * (flux - mean[None, :])
    scale = lax.rsqrt(jnp.sum(resid * resid, axis=1) / PIX + 1e-06)
    ready = (resid * scale[:, None]).astype(BF16)
    ready = ready.reshape(rows, R, Q).transpose(2, 0, 1)
    gathered = lax.all_gather(ready, "blk", axis=1, tiled=True)
    return correlate(x, gathered, exposure_per_row)


def solution(mesh):
    in_specs = (
        P(("grp", "blk"), None),
        P(("grp", "blk"), None),
        P(("grp", "blk"), None),
        P(("grp", "blk")),
        P(),
        P("grp"),
    )
    out_specs = P("grp", "blk")
    return jax.shard_map(
        functools.partial(shards, mesh.shape["blk"]),
        mesh=mesh,
        in_specs=in_specs,
        out_specs=out_specs,
        check_vma=False,
    )
```

```python
import functools
import math

import jax
import jax.numpy as jnp
from jax import lax
from jax.experimental import pallas as pl
from jax.experimental.pallas import tpu as pltpu
from jax.sharding import PartitionSpec as P

PIX = 16384
LAGS = 64
TAPS = 97
KERNELS = 8
Q = 128
R = PIX // Q
BAND = 640
CHUNKS = 8
LEAD = 4
AHEAD = 7
PIECES = ((0, 4), (4, 6), (6, 8))
F32 = jnp.float32
BF16 = jnp.bfloat16
MESH = pl.DeviceIdType.MESH
NT_DIMS = (((1,), (1,)), ((), ()))


def template_kernel(index_ref, table_ref, templates_ref, x_ref, bands, chunks, smooth):
    count = templates_ref.shape[0]
    spread_templates(table_ref, templates_ref, bands, chunks)
    smooth_templates(index_ref, bands, chunks, smooth, 0, count, count)
    pack_templates(smooth, x_ref, count)


def spread_templates(table_ref, templates_ref, bands, chunks):
    count = templates_ref.shape[0]
    for k in range(KERNELS):
        row = jnp.concatenate(
            [table_ref[k : k + 1, :], jnp.zeros((1, BAND - TAPS), F32)], axis=1
        )
        row = jnp.broadcast_to(row, (Q, BAND))
        band = pltpu.roll(row, 0, 1, stride=4, stride_axis=0)
        high = band.astype(BF16)
        bands[k, :, :BAND] = high
        bands[k, :, BAND:] = (band - high.astype(F32)).astype(BF16)

    def spread(r, _):
        at = pl.multiple_of(r * (4 * Q), 128)
        piece = templates_ref[:, pl.ds(at, BAND)].astype(F32)
        for i in range(BAND // 128):
            chunks[i, pl.ds(pl.multiple_of(r * count, count), count), :] = piece[
                :, 128 * i : 128 * (i + 1)
            ]
        return 0

    lax.fori_loop(0, R - 1, spread, 0, unroll=8)
    last = (R - 1) * 4 * Q
    left = templates_ref.shape[1] - last
    tail = templates_ref[:, last:].astype(F32)
    tail = jnp.concatenate([tail, jnp.zeros((count, BAND - left), F32)], axis=1)
    for i in range(BAND // 128):
        chunks[i, (R - 1) * count :, :] = tail[:, 128 * i : 128 * (i + 1)]


def smooth_templates(index_ref, bands, chunks, smooth, first, last, count):
    for t in range(first, last):
        rows = [
            chunks[i, pl.ds(t, R, stride=count), :].astype(BF16) for i in range(BAND // 128)
        ]
        rows = jnp.concatenate(rows + rows, axis=1)
        flux = lax.dot_general(
            bands[index_ref[t]], rows, NT_DIMS, preferred_element_type=F32
        )
        total = jnp.sum(flux * flux)
        smooth[pl.ds(t, Q, stride=count), :] = flux * lax.rsqrt(
            jnp.full((1, 1), total) / PIX + 1e-06
        )


def pack_templates(smooth, x_ref, count):
    half = LAGS // 2
    body = smooth[...]
    lane = lax.broadcasted_iota(jnp.int32, (half * count, R), 1)
    x_ref[half * count : (half + Q) * count, :] = body.astype(BF16)
    before = pltpu.roll(body[(Q - half) * count :, :], 1, 1)
    x_ref[: half * count, :] = jnp.where(lane == 0, 0.0, before).astype(BF16)
    after = pltpu.roll(body[: half * count, :], R - 1, 1)
    x_ref[(half + Q) * count :, :] = jnp.where(lane == R - 1, 0.0, after).astype(BF16)


def shape_templates(templates, template_kernel_index, line_spread_table):
    count = templates.shape[0]
    return pl.pallas_call(
        template_kernel,
        out_shape=jax.ShapeDtypeStruct(((Q + LAGS) * count, R), BF16),
        in_specs=[
            pl.BlockSpec(memory_space=pltpu.SMEM),
            pl.BlockSpec(memory_space=pltpu.VMEM),
            pl.BlockSpec(memory_space=pltpu.VMEM),
        ],
        out_specs=pl.BlockSpec(memory_space=pltpu.VMEM),
        scratch_shapes=[
            pltpu.VMEM((KERNELS, Q, 2 * BAND), BF16),
            pltpu.VMEM((BAND // 128, R * count, 128), F32),
            pltpu.VMEM((Q * count, R), F32),
        ],
        compiler_params=pltpu.CompilerParams(vmem_limit_bytes=40 * 2**20),
        cost_estimate=pl.CostEstimate(
            flops=2 * count * Q * R * 2 * BAND, bytes_accessed=6 * 2**20, transcendentals=0
        ),
        name="shape_templates",
    )(template_kernel_index, line_spread_table, templates)


def place_rows(rows_ref, acc, out_ref, count, group=0, groups=1):
    total_rows = rows_ref.shape[1]
    chosen = (
        lax.broadcasted_iota(jnp.int32, (total_rows, total_rows), 0) == rows_ref[...]
    ).astype(BF16)
    both = jnp.concatenate([chosen, chosen], axis=1)
    for t in range(group * count // groups, (group + 1) * count // groups, 2):
        part = jnp.concatenate(
            [
                jnp.concatenate(
                    [
                        acc[h, pl.ds(t + i, LAGS, stride=count), :]
                        for h in range(total_rows // 128)
                    ],
                    axis=1,
                )
                for i in range(2)
            ],
            axis=0,
        ) * F32(1.0 / math.sqrt(PIX))
        high = part.astype(BF16)
        low = (part - high.astype(F32)).astype(BF16)
        out_ref[:, t * LAGS : (t + 2) * LAGS] = lax.dot_general(
            both,
            jnp.concatenate([high, low], axis=1),
            NT_DIMS,
            preferred_element_type=F32,
        )


def correlate_kernel(step_q, rows_ref, x_ref, g_ref, out_ref, acc):
    step = pl.program_id(0)
    total_rows = rows_ref.shape[1]
    count = x_ref.shape[0] // (Q + LAGS)
    tile = 256

    @pl.when(step == 0)
    def _():
        acc[...] = jnp.zeros_like(acc)

    right = jnp.concatenate([g_ref[i] for i in range(step_q)], axis=1)
    for m in range(LAGS * count // tile):
        left = jnp.concatenate(
            [
                x_ref[pl.ds(pl.multiple_of((step * step_q + i) * count + m * tile, 16), tile), :]
                for i in range(step_q)
            ],
            axis=1,
        )
        part = lax.dot_general(left, right, NT_DIMS, preferred_element_type=F32)
        for h in range(total_rows // 128):
            acc[h, m * tile : (m + 1) * tile, :] += part[:, 128 * h : 128 * (h + 1)]

    @pl.when(step == pl.num_programs(0) - 1)
    def _():
        place_rows(rows_ref, acc, out_ref, count)


def correlate(x, gathered, exposure_per_row):
    total_rows = gathered.shape[1]
    count = x.shape[0] // (Q + LAGS)
    step_q = 8
    return pl.pallas_call(
        functools.partial(correlate_kernel, step_q),
        grid=(Q // step_q,),
        out_shape=jax.ShapeDtypeStruct((total_rows, count * LAGS), F32),
        in_specs=[
            pl.BlockSpec((1, total_rows), lambda s: (0, 0)),
            pl.BlockSpec(x.shape, lambda s: (0, 0)),
            pl.BlockSpec((step_q, total_rows, R), lambda s: (s, 0, 0)),
        ],
        out_specs=pl.BlockSpec((total_rows, count * LAGS), lambda s: (0, 0)),
        scratch_shapes=[pltpu.VMEM((total_rows // 128, LAGS * count, 128), F32)],
        compiler_params=pltpu.CompilerParams(vmem_limit_bytes=40 * 2**20),
        name="correlate",
    )(exposure_per_row.reshape(1, total_rows), x, gathered)


def column_sums(mine, psum):
    kind = lax.broadcasted_iota(jnp.int32, (16, 256), 0)
    lane = lax.broadcasted_iota(jnp.int32, (16, 256), 1)
    pick = (lane // 16 == kind).astype(BF16)
    for j in range(Q // 16):
        part = mine[16 * j : 16 * (j + 1)].reshape(256, R)
        good = (part.astype(F32) > 0).astype(BF16)
        for i, what in enumerate((part, good)):
            psum[j // 4, i, 16 * (j % 4) : 16 * (j % 4 + 1), :] = lax.dot_general(
                pick, what, (((1,), (0,)), ((), ())), preferred_element_type=F32
            )


def row_scales(mine, means):
    zero = jnp.zeros((16, R), F32)

    def add(j, total):
        for i in range(16):
            flux = mine[16 * j + i].astype(F32)
            resid = jnp.where(flux > 0, flux - means[j, i : i + 1, :], 0.0)
            total = total + resid * resid
        return total

    total = lax.fori_loop(0, Q // 16, add, zero)
    return lax.rsqrt(jnp.sum(total, axis=1, keepdims=True) / PIX + 1e-06)


def diagonal():
    row = lax.broadcasted_iota(jnp.int32, (16, R), 0)
    lane = lax.broadcasted_iota(jnp.int32, (16, R), 1)
    return row == lane


def store_body(smooth, x, count):
    x[0, LAGS // 2 : LAGS // 2 + Q] = smooth[...].reshape(Q, count, R).astype(BF16)


def store_margins(x, tt):
    half = LAGS // 2
    count = x.shape[2]
    lane = lax.broadcasted_iota(jnp.int32, (half * count, R), 1)

    def rolled(first, shift, edge):
        part = x[tt, first : first + half].reshape(half * count, R).astype(F32)
        part = jnp.where(lane == edge, 0.0, pltpu.roll(part, shift, 1))
        return part.astype(BF16).reshape(half, count, R)

    x[tt, :half] = rolled(Q, 1, 0)
    x[tt, half + Q :] = rolled(half, R - 1, R - 1)


def cross_kernel(
    mine,
    index_ref,
    table_ref,
    templates_ref,
    out_ref,
    raw,
    ready,
    x,
    partner,
    psum,
    tsum,
    csum,
    rsum,
    means,
    row_scale,
    scale,
    bands,
    chunks,
    smooth,
    raw_send,
    raw_recv,
    x_sem,
    r_send,
    r_recv,
    t_sem,
    s_send,
    s_recv,
    m_send,
    m_recv,
    v_send,
    v_recv,
    tail,
    tail_sem,
):
    me = lax.axis_index("blk")
    z, y, c = me // 4, (me // 2) % 2, me % 2
    planes = 4
    count = templates_ref.shape[0]
    span = Q // CHUNKS

    def blk(zz, yy, cc):
        return (zz * 2 + yy) * 2 + cc

    up, down = blk(z + 1, y, c), blk(z - 1, y, c)
    beside, twin = blk(z, 1 - y, c), blk(z, y, 1 - c)
    middle = (z == 1) | (z == 2)
    has_up, has_down = z < planes - 1, z > 0

    def remote(src, dst, send, recv, to):
        return pltpu.make_async_remote_copy(
            src_ref=src,
            dst_ref=dst,
            send_sem=send,
            recv_sem=recv,
            device_id={"blk": to},
            device_id_type=MESH,
        )

    barrier = pltpu.get_barrier_semaphore()

    def greet(o, _):
        pl.semaphore_signal(
            barrier, inc=1, device_id={"blk": lax.rem(me + o, 16)}, device_id_type=MESH
        )
        return 0

    lax.fori_loop(1, 16, greet, 0)
    raw[z, c] = mine[...]
    pl.semaphore_wait(barrier, 15)

    def raw_copy(zs, k, kind, to):
        part = raw.at[zs, c, pl.ds(k * span, span)]
        return remote(
            part, part, raw_send.at[kind, zs, k], raw_recv.at[zs * 2 + c, k], to
        )

    def from_twin(zs, k):
        part = raw.at[zs, 1 - c, pl.ds(k * span, span)]
        remote(
            part, part, raw_send.at[2, zs, k], raw_recv.at[zs * 2 + 1 - c, k], twin
        ).wait_recv()

    def on_sides(h, act):
        for sign in (1, -1):
            zs = z + sign * h
            pl.when((zs >= 0) & (zs < planes))(functools.partial(act, zs, sign))

    def send(s):
        h, k = s // CHUNKS, s % CHUNKS
        if h == 0:
            pl.when(has_up)(lambda: raw_copy(z, k, 0, up).start())
            pl.when(has_down)(lambda: raw_copy(z, k, 1, down).start())
            raw_copy(z, k, 2, twin).start()
        elif h < planes - 1:

            def onward(zs, sign):
                if sign > 0:
                    pl.when(has_down)(lambda: raw_copy(zs, k, 1, down).start())
                else:
                    pl.when(has_up)(lambda: raw_copy(zs, k, 0, up).start())

            on_sides(h, onward)

    def arrive(s):
        h, k = s // CHUNKS + 1, s % CHUNKS

        def land(zs, sign):
            raw_copy(zs, k, 2, twin).wait_recv()
            raw_copy(zs, k, 2, twin).start()

        on_sides(h, land)

    def step(s, lead):
        arrive(s)
        send(s + lead)

    send(0)
    send(1)

    column_sums(mine, psum)
    to_twin = remote(psum.at[1 - c], tsum, t_sem.at[0], t_sem.at[1], twin)
    to_twin.start()
    spread_templates(table_ref, templates_ref, bands, chunks)

    def owner(w):
        return blk(1 + w // 2, w % 2, c)

    def sum_copy(w):
        return remote(
            csum.at[w], rsum.at[z * 2 + y], s_send.at[w], s_recv.at[z * 2 + y], owner(w)
        )

    def sum_from(i):
        return remote(csum.at[0], rsum.at[i], s_send.at[0], s_recv.at[i], twin)

    def mean_copy(w, o):
        part = means.at[4 * c + w]
        chip = lax.rem(z * 2 + y + o, 8)
        return remote(
            part, part, m_send.at[o], m_recv.at[w], blk(chip // 2, chip % 2, c)
        )

    mine_w = (z - 1) * 2 + y

    def sums_to_owners():
        to_twin.wait_recv()
        for w in range(4):
            rows = slice(16 * w, 16 * (w + 1))
            csum[w] = psum[c, :, rows, :] + tsum[:, rows, :]
            away = jnp.logical_not(middle & (mine_w == w))
            pl.when(away)(lambda: sum_copy(w).start())

            @pl.when(jnp.logical_not(away))
            def _():
                rsum[z * 2 + y] = csum[w]

    def means_from_owner():
        @pl.when(middle)
        def _():
            for i in range(8):
                pl.when(z * 2 + y != i)(lambda: sum_from(i).wait_recv())
            total = rsum[0]
            for i in range(1, 8):
                total = total + rsum[i]
            means[4 * c + mine_w] = total[0] / jnp.maximum(total[1], 1.0)
            for o in range(1, 8):
                mean_copy(mine_w, o).start()

    half_means = remote(
        means.at[pl.ds(4 * c, 4)],
        means.at[pl.ds(4 * c, 4)],
        t_sem.at[2],
        t_sem.at[3],
        twin,
    )

    def means_to_twin():
        for w in range(4):
            away = jnp.logical_not(middle & (mine_w == w))
            pl.when(away)(lambda: mean_copy(w, 1).wait_recv())
        half_means.start()

    def scale_copy(o):
        at = lax.rem(z * 2 + c + o, 8)
        return remote(
            row_scale.at[z * 2 + c],
            row_scale.at[z * 2 + c],
            v_send.at[o],
            v_recv.at[z * 2 + c],
            blk(at // 2, y, at % 2),
        )

    def scales_out():
        half_means.wait_recv()
        own = row_scales(mine, means)
        row_scale[z * 2 + c] = jnp.sum(
            jnp.where(diagonal(), own, 0.0), axis=0, keepdims=True
        )
        for o in range(1, 8):
            scale_copy(o).start()

    def scales_in():
        for i in range(8):
            part = row_scale.at[i]
            pl.when(z * 2 + c != i)(
                lambda: remote(part, part, v_send.at[0], v_recv.at[i], twin).wait_recv()
            )
            column = jnp.sum(
                jnp.where(diagonal(), row_scale[i], 0.0), axis=1, keepdims=True
            )
            scale[i] = jnp.broadcast_to(column, (16, R))

    def x_copy(k):
        rows = pl.ds(LAGS // 2 + k * span, span)
        return remote(
            x.at[0, rows], x.at[1, rows], x_sem.at[0, k], x_sem.at[1, k], beside
        )

    smooth_templates(index_ref, bands, chunks, smooth, 0, 2, count)
    sums_to_owners()
    send(2)
    send(3)
    smooth_templates(index_ref, bands, chunks, smooth, 2, count, count)
    store_body(smooth, x, count)
    x_copy(0).start()
    for zs in range(planes):
        ready[zs, :AHEAD] = jnp.zeros((AHEAD, 32, R), BF16)
        ready[zs, AHEAD + Q :] = jnp.zeros((ready.shape[1] - AHEAD - Q, 32, R), BF16)
    store_margins(x, 0)
    after = {2: means_from_owner, 5: means_to_twin, 6: scales_out, 9: scales_in}
    for s in range(10):
        step(s, LEAD if s < 8 else 8)
        if 0 < s + 1 < CHUNKS:
            x_copy(s + 1).start()
        after.get(s, lambda: None)()
        if s == 7:
            for e in range(8 + LEAD, 8 + 8):
                send(e)

    def normalise(zs, first, last):
        for cc in range(2):
            factor = scale[zs * 2 + cc]

            def tile(j, _):
                for i in range(16):
                    flux = raw[zs, cc, 16 * j + i].astype(F32)
                    resid = jnp.where(flux > 0, flux - means[j, i : i + 1, :], 0.0)
                    ready[zs, AHEAD + 16 * j + i, 16 * cc : 16 * (cc + 1), :] = (
                        resid * factor
                    ).astype(BF16)
                return 0

            lax.fori_loop(first, last, tile, 0)

    def product(zs, first, last, ends=False):
        right = jnp.concatenate(
            [ready[zs, i : i + 8].reshape(256, R) for i in range(first, last)], axis=1
        )
        left = jnp.concatenate(
            [
                jnp.concatenate(
                    [x[tt, i + 8 * a] for tt in range(2) for a in range(8)], axis=0
                )
                for i in range(first, last)
            ],
            axis=1,
        )
        part = lax.dot_general(left, right, NT_DIMS, preferred_element_type=F32)
        if ends:
            out_ref[zs * 2 + y] += part[:128]
            tail[0] = part[128:].astype(BF16)
        elif first == 0:
            out_ref[zs * 2 + y] = part[:128]
            partner[zs] = part[128:]
        else:
            out_ref[zs * 2 + y] += part[:128]
            partner[zs] += part[128:]

    def result_copy(zs):
        return remote(
            partner.at[zs], out_ref.at[zs * 2 + y], r_send.at[zs], r_recv.at[zs], beside
        )

    def slot(i):
        near = jnp.where(z < 2, z + 1, z - 1)
        far = jnp.where(z == 0, 2, jnp.where(z == 1, 0, jnp.where(z == 2, 3, 1)))
        end = jnp.where(z < 2, 3, 0)
        return jnp.where(
            i == 0, z, jnp.where(i == 1, near, jnp.where(i == 2, far, end))
        )

    def block(i, _):
        zs = slot(i)

        @pl.when(i == 1)
        def _():
            for s in range(10, 14):
                step(s, 8)

        @pl.when(i == 2)
        def _():
            for s in range(14, 16):
                step(s, 8)

        for k in range(CHUNKS):
            from_twin(zs, k)
        normalise(zs, 0, Q // 16)

        @pl.when(i == 0)
        def _():
            for k in range(CHUNKS):
                x_copy(k).wait_recv()
            store_margins(x, 1)

        @pl.when(z < planes)
        def _():
            for quarter in range(4):
                product(zs, 32 * quarter, 32 * quarter + (32 if quarter < 3 else 40))

        result_copy(zs).start()
        return 0

    lax.fori_loop(0, 3, block, 0)
    last = slot(3)
    for first, end in PIECES:
        for k in range(first, end):
            arrive(16 + k)
            if k > first:
                from_twin(last, k - 1)
                normalise(last, k - 1, k)
        from_twin(last, end - 1)
        normalise(last, end - 1, end)
        ends = end == CHUNKS
        low, high = span * first, span * end + (8 if ends else 0)
        pl.when(z < planes)(functools.partial(product, last, low, high, ends))
        if first == PIECES[-2][0]:
            result_copy(last).start()
    tail_copy = remote(tail.at[0], tail.at[1], tail_sem.at[0], tail_sem.at[1], beside)
    tail_copy.start()

    for k in range(CHUNKS):
        x_copy(k).wait_send()
    to_twin.wait_send()
    half_means.wait_send()
    for w in range(4):
        away = jnp.logical_not(middle & (mine_w == w))
        pl.when(away)(lambda: sum_copy(w).wait_send())

    @pl.when(middle)
    def _():
        for o in range(1, 8):
            mean_copy(mine_w, o).wait_send()

    for o in range(1, 8):
        scale_copy(o).wait_send()

    def sent(k, _):
        for zs in range(planes):
            raw_copy(zs, k, 2, twin).wait_send()
            pl.when(has_up & (zs <= z))(lambda: raw_copy(zs, k, 0, up).wait_send())
            pl.when(has_down & (zs >= z))(lambda: raw_copy(zs, k, 1, down).wait_send())
        return 0

    lax.fori_loop(0, CHUNKS, sent, 0)
    for zs in range(planes):
        result_copy(zs).wait_send()
    tail_copy.wait_send()
    for zs in range(planes):
        result_copy(zs).wait_recv()
    tail_copy.wait_recv()
    out_ref[last * 2 + 1 - y] += tail[1].astype(F32)


def cross(masked, templates, template_kernel_index, line_spread_table):
    count = templates.shape[0]
    rows = masked.shape[1]
    vmem = pl.BlockSpec(memory_space=pltpu.VMEM)
    dma = pltpu.SemaphoreType.DMA
    return pl.pallas_call(
        cross_kernel,
        out_shape=jax.ShapeDtypeStruct((8, 8 * count, 256), F32),
        in_specs=[vmem, pl.BlockSpec(memory_space=pltpu.SMEM), vmem, vmem],
        out_specs=vmem,
        scratch_shapes=[
            pltpu.VMEM((4, 2, Q, rows, R), BF16),
            pltpu.VMEM((4, Q + 16, 2 * rows, R), BF16),
            pltpu.VMEM((2, Q + LAGS, count, R), BF16),
            pltpu.VMEM((4, 8 * count, 256), F32),
            pltpu.VMEM((2, 2, Q // 2, R), F32),
            pltpu.VMEM((2, Q // 2, R), F32),
            pltpu.VMEM((4, 2, 16, R), F32),
            pltpu.VMEM((8, 2, 16, R), F32),
            pltpu.VMEM((8, 16, R), F32),
            pltpu.VMEM((8, 1, R), F32),
            pltpu.VMEM((8, 16, R), F32),
            pltpu.VMEM((KERNELS, Q, 2 * BAND), BF16),
            pltpu.VMEM((BAND // 128, R * count, 128), F32),
            pltpu.VMEM((Q * count, R), F32),
            dma((3, 4, CHUNKS)),
            dma((8, CHUNKS)),
            dma((2, CHUNKS)),
            dma((4,)),
            dma((4,)),
            dma((4,)),
            dma((4,)),
            dma((8,)),
            dma((8,)),
            dma((4,)),
            dma((8,)),
            dma((8,)),
            pltpu.VMEM((2, 8 * count, 256), BF16),
            dma((2,)),
        ],
        compiler_params=pltpu.CompilerParams(
            collective_id=0, has_side_effects=True, vmem_limit_bytes=48 * 2**20
        ),
        name="cross",
    )(masked, template_kernel_index, line_spread_table, templates)


def place_kernel(rows_ref, part_ref, out_hbm, split, out_ref, sem):
    count = part_ref.shape[1] // 8
    lane = lax.broadcasted_iota(jnp.int32, (8 * count, 128), 1) // 32
    for h in range(2):
        for b in range(8):
            at = 7 - b
            piece = None
            for i in range(4):
                one = part_ref[4 * h + i, :, 128 * (at // 4) : 128 * (at // 4 + 1)]
                shift = 32 * (i - at % 4) % 128
                one = pltpu.roll(one, shift, 1) if shift else one
                piece = one if piece is None else jnp.where(lane == i, one, piece)
            for a in range(8):
                split[h, (8 * a + b) * count : (8 * a + b + 1) * count, :] = piece[
                    a * count : (a + 1) * count
                ]
    groups = sem.shape[0]
    wide = out_ref.shape[1] // groups
    copies = []
    for g in range(groups):
        place_rows(rows_ref, split, out_ref, count, g, groups)
        at = pl.ds(g * wide, wide)
        copies.append(
            pltpu.make_async_copy(out_ref.at[:, at], out_hbm.at[:, at], sem.at[g])
        )
        copies[-1].start()
    for copy in copies:
        copy.wait()


def place(parts, exposure_per_row):
    total_rows = 32 * parts.shape[0]
    across = parts.shape[1] * 8
    return pl.pallas_call(
        place_kernel,
        out_shape=jax.ShapeDtypeStruct((total_rows, across), F32),
        in_specs=[pl.BlockSpec(memory_space=pltpu.VMEM)] * 2,
        out_specs=pl.BlockSpec(memory_space=pl.ANY),
        scratch_shapes=[
            pltpu.VMEM((total_rows // 128, across, 128), F32),
            pltpu.VMEM((total_rows, across), F32),
            pltpu.SemaphoreType.DMA((4,)),
        ],
        compiler_params=pltpu.CompilerParams(vmem_limit_bytes=16 * 2**20),
        name="place",
    )(exposure_per_row.reshape(1, total_rows), parts)


def shards(
    devices,
    observed,
    good_pixel_mask,
    templates,
    template_kernel_index,
    line_spread_table,
    exposure_per_row,
):
    rows = observed.shape[0]
    flux = jnp.where(good_pixel_mask > 0, observed, 0)
    if devices == 16 and rows == 16 and templates.shape[0] == 16:
        masked = flux.reshape(rows, R, Q).transpose(2, 0, 1)
        parts = cross(masked, templates, template_kernel_index, line_spread_table)
        return place(parts, exposure_per_row)
    flux = flux.astype(F32)
    present = (flux > 0).astype(F32)
    sums, counts = jnp.sum(flux, axis=0), jnp.sum(present, axis=0)
    x = shape_templates(templates, template_kernel_index, line_spread_table)
    sums = lax.psum(jnp.stack([sums, counts]), "blk")
    mean = sums[0] / jnp.maximum(sums[1], 1.0)
    resid = present * (flux - mean[None, :])
    scale = lax.rsqrt(jnp.sum(resid * resid, axis=1) / PIX + 1e-06)
    ready = (resid * scale[:, None]).astype(BF16)
    ready = ready.reshape(rows, R, Q).transpose(2, 0, 1)
    gathered = lax.all_gather(ready, "blk", axis=1, tiled=True)
    return correlate(x, gathered, exposure_per_row)


def solution(mesh):
    in_specs = (
        P(("grp", "blk"), None),
        P(("grp", "blk"), None),
        P(("grp", "blk"), None),
        P(("grp", "blk")),
        P(),
        P("grp"),
    )
    out_specs = P("grp", "blk")
    return jax.shard_map(
        functools.partial(shards, mesh.shape["blk"]),
        mesh=mesh,
        in_specs=in_specs,
        out_specs=out_specs,
        check_vma=False,
    )
```
